256 devices in a mesh: group: 4 (over y), tp: 32 (over z, x), dec: 2 (over core).
Axes of the slice: x: 4, y: 4, z: 8, core: 2. Of those that a mesh axis runs over, the one named last changes fastest.
Arguments:
- hidden: bfloat16 [3072, 7168], P(('group', 'dec'), 'tp'), may hold values from -6 to 6
- in_gain: bfloat16 [7168], P('tp'), may hold values from 0.099609375 to 1.8984375
- kv_weight: bfloat16 [7168, 576], P('tp'), may hold values from -0.0625 to 0.0625
- kv_gain: bfloat16 [512], replicated, may hold values from 0.099609375 to 1.8984375
- span_req: int32 [8], replicated, may hold values from 0 to 95, as said below
- lengths: int32 [96], replicated, may hold values from 384 to 16384, as said below
- cache: bfloat16 [96, 16384, 576], P(('group', 'dec'), 'tp'), may hold values from -8 to 8
- q_nope: bfloat16 [96, 4, 128, 128], P(('group', 'dec'), None, 'tp'), may hold values from -6 to 6
- q_rope: bfloat16 [96, 4, 128, 64], P(('group', 'dec'), None, 'tp'), may hold values from -8 to 8
- new_latent: bfloat16 [96, 4, 576], P(('group', 'dec')), may hold values from -8 to 8
- key_absorb: bfloat16 [128, 128, 512], P('tp'), may hold values from -0.5 to 0.5
- value_absorb: bfloat16 [128, 512, 128], P('tp'), may hold values from -0.25 to 0.25
Outputs:
- new_rows: bfloat16 [3072, 576], P(('group', 'dec'))
- attended: bfloat16 [96, 4, 128, 128], P(('group', 'dec'), None, 'tp')
The draws below stay inside these ranges and needn't reach their ends.
Inputs may be any that keep to these rules, and one draw needn't show every extreme that they name: `span_req`: distinct request ids, each in 0 to 95; request r is held by index r // 12 of group+dec, and no two spans go to requests of the same index. Requests named in span_req have lengths of at most 768.
All inputs are finite; a program needn't handle non-finite values.
Results may differ from the reference program's by a relative error of at most 0.025.
Values may be sent and summed in bfloat16 or wider, within the bound.
No kernel may reach another device: no remote copies, remote signals or barrier semaphores. Data moves between devices by JAX's collectives and lax.ppermute only.
A program may use at most 128 MiB of HBM per device.

```python
import math
import jax
import jax.numpy as jnp
from jax import lax

D = 7168
H = 128
LAT = 512
NOPE = 128
ROPE = 64
VHEAD = 128
R_DEV = 12
LSEG = 512
SPAN = 384
STEPS = 4
PRE = 8
REQ = 96
CACHE = 16384


def span_plan(key):
    plan_key = jax.random.fold_in(key, 700)
    key_perm, key_pick, key_slot = jax.random.split(plan_key, 3)
    owners = jax.random.permutation(key_perm, PRE).astype(jnp.int32)
    picked = jax.random.randint(key_pick, (), 0, PRE).astype(jnp.int32)
    target = (picked + PRE // 2) % PRE
    place = jnp.sum(jnp.where(owners == target, jnp.arange(PRE, dtype=jnp.int32), 0)).astype(jnp.int32)
    displaced = owners[picked]
    owners = owners.at[place].set(displaced).at[picked].set(target)
    slots = jax.random.randint(key_slot, (PRE,), 0, R_DEV).astype(jnp.int32)
    request_ids = owners * R_DEV + slots
    return (request_ids, picked, owners, slots)


def length_plan(key):
    request_ids, picked, owners, slots = span_plan(key)
    plan_key = jax.random.fold_in(key, 717)
    key_values, key_span, key_long = jax.random.split(plan_key, 3)
    values = jax.random.randint(key_values, (REQ,), SPAN, CACHE + 1).astype(jnp.int32)
    span_lengths = jax.random.randint(key_span, (PRE,), SPAN, 2 * SPAN + 1).astype(jnp.int32)
    values = values.at[request_ids].set(span_lengths)
    values = values.at[request_ids[picked]].set(SPAN)
    long_owner = jax.random.randint(key_long, (), 0, PRE).astype(jnp.int32)
    longest = owners[long_owner] * R_DEV + (slots[long_owner] + 1) % R_DEV
    values = values.at[longest].set(CACHE)
    return values.astype(jnp.int32)


def draw_q_rope(key, part):
    key = jax.random.fold_in(key, 11)
    values = jnp.clip(jax.random.normal(key, (REQ, STEPS, H, ROPE)), -6.0, 6.0)
    return values.astype(jnp.bfloat16)


def draw_new_latent(key, part):
    key = jax.random.fold_in(key, 13)
    values = jnp.clip(jax.random.normal(key, (REQ, STEPS, LAT + ROPE)), -6.0, 6.0)
    return values.astype(jnp.bfloat16)


def draw_cache(key, part):
    key = jax.random.fold_in(key, 19)
    values = jnp.clip(jax.random.normal(key, (REQ, CACHE, LAT + ROPE)), -6.0, 6.0)
    return values.astype(jnp.bfloat16)


def draw_lengths(key, part):
    values = length_plan(key)
    return values.astype(jnp.int32)


def draw_span_req(key, part):
    request_ids, picked, owners, slots = span_plan(key)
    return request_ids.astype(jnp.int32)


def block_scale(rng, extent, cuts, least, top_value):
    level = 1.0
    for dim, parts in cuts:
        heights = jax.random.uniform(jax.random.fold_in(jax.random.fold_in(rng, 6), dim), (parts,), jnp.float32, least / len(cuts), top_value / len(cuts))
        level = level * jnp.repeat(jnp.exp(heights), extent[dim] // parts).reshape((-1,) + (1,) * (len(extent) - 1 - dim))
    return level


def gaussian(key, shape, scale, reach, shards=(), kind=jnp.bfloat16):
    loudness = block_scale(key, shape, shards, -0.22, 0.18) if shards else 1.0
    entries = jax.random.normal(key, shape, jnp.float32) * scale * loudness
    return jnp.minimum(jnp.maximum(entries, -reach), reach).astype(kind)


def setup_inputs(seed: int = 0) -> dict:
    seeds = jax.random.split(jax.random.key(seed), 13)
    hidden = gaussian(seeds[0], (PRE * SPAN, D), 1.0, 6.0, ((0, 8), (1, 32)))
    in_gain = jnp.clip(1.0 + 0.18 * jax.random.normal(seeds[1], (D,), jnp.float32), 0.099609375, 1.8984375).astype(jnp.bfloat16)
    kv_weight = gaussian(seeds[2], (D, LAT + ROPE), D ** -0.5, 0.0625, ((0, 32),))
    kv_gain = jnp.clip(1.0 + 0.18 * jax.random.normal(seeds[3], (LAT,), jnp.float32), 0.099609375, 1.8984375).astype(jnp.bfloat16)
    span_req = draw_span_req(jax.random.fold_in(seeds[12], 71), 0)
    lengths = draw_lengths(jax.random.fold_in(seeds[12], 71), 0)
    cache = draw_cache(jax.random.fold_in(seeds[12], 71), 0)
    q_nope = gaussian(seeds[7], (REQ, STEPS, H, NOPE), 1.0, 6.0, ((0, 8), (2, 32)))
    q_rope = draw_q_rope(jax.random.fold_in(seeds[12], 71), 0)
    new_latent = draw_new_latent(jax.random.fold_in(seeds[12], 71), 0)
    key_absorb = gaussian(seeds[10], (H, NOPE, LAT), NOPE ** -0.5, 0.5, ((0, 32),))
    value_absorb = gaussian(seeds[11], (H, LAT, VHEAD), LAT ** -0.5, 0.25, ((0, 32),))
    return dict(hidden=hidden, in_gain=in_gain, kv_weight=kv_weight, kv_gain=kv_gain, span_req=span_req, lengths=lengths, cache=cache, q_nope=q_nope, q_rope=q_rope, new_latent=new_latent, key_absorb=key_absorb, value_absorb=value_absorb)


EPSILON = 1e-06

def rotate_pair(values, positions):
    half_width = values.shape[-1] // 2
    index_list = jnp.arange(half_width, dtype=jnp.float32)
    frequency = jnp.exp(index_list * (-math.log(10000.0) / half_width))
    angles = positions.astype(jnp.float32)[:, None] * frequency[None, :]
    cosine = jnp.cos(angles)
    sine_part = jnp.sin(angles)
    first_half = values[:, :half_width]
    second_half = values[:, half_width:]
    return jnp.concatenate([first_half * cosine - second_half * sine_part, first_half * sine_part + second_half * cosine], -1)

def finish_rows(projected, squares, positions, kv_gain):
    latent_width = kv_gain.shape[0]
    projected = projected * lax.rsqrt(squares / D + EPSILON)[:, None]
    latent = projected[:, :latent_width]
    latent = latent * lax.rsqrt(lax.optimization_barrier(jnp.mean(latent * latent, -1, keepdims=True)) + EPSILON) * kv_gain.astype(jnp.float32)
    return jnp.concatenate([latent, rotate_pair(projected[:, latent_width:], positions)], -1).astype(jnp.bfloat16)

def reference(hidden, in_gain, kv_weight, kv_gain, span_req, lengths, cache, q_nope, q_rope, new_latent, key_absorb, value_absorb):
    produced = []
    for source in range(PRE):
        span_hidden = hidden[source * SPAN:(source + 1) * SPAN].astype(jnp.float32)
        scaled = (span_hidden * in_gain.astype(jnp.float32)).astype(jnp.bfloat16)
        projected = jnp.dot(scaled, kv_weight, preferred_element_type=jnp.float32)
        squares = lax.optimization_barrier(jnp.sum(span_hidden * span_hidden, -1))
        request_id = span_req[source].astype(jnp.int32)
        offset = (lengths[request_id] - SPAN).astype(jnp.int32)
        positions = offset + jnp.arange(SPAN, dtype=jnp.int32)
        span_rows = finish_rows(projected, squares, positions, kv_gain)
        produced.append(span_rows)
        cache = lax.dynamic_update_slice(cache, span_rows[None], (request_id, offset, jnp.int32(0)))
    new_rows = jnp.concatenate(produced, 0)
    q_latent = jnp.einsum('rshn,hnc->rshc', q_nope.astype(jnp.float32), key_absorb.astype(jnp.float32)).astype(jnp.bfloat16)
    query_all = jnp.concatenate([q_latent, q_rope], -1)
    score_scale = 1.0 / math.sqrt(NOPE + ROPE)
    causal = jnp.arange(STEPS, dtype=jnp.int32)[None, :] <= jnp.arange(STEPS, dtype=jnp.int32)[:, None]
    value_float = value_absorb.astype(jnp.float32)
    block_count = CACHE // LSEG

    def attend(request_items):
        query_rows, cache_rows, fresh_rows, length = request_items
        query_float = query_rows.astype(jnp.float32)
        cache_float = cache_rows.astype(jnp.float32)
        fresh_float = fresh_rows.astype(jnp.float32)
        scores = jnp.einsum('shc,pc->shp', query_float, cache_float) * score_scale
        valid_keys = jnp.arange(CACHE, dtype=jnp.int32) < length
        scores = jnp.where(valid_keys[None, None, :], scores, -1e+30)
        scores = scores.reshape(STEPS, H, block_count, LSEG)
        block_top = lax.optimization_barrier(jnp.max(scores, -1))
        weights = jnp.exp(scores - block_top[..., None]).astype(jnp.bfloat16).astype(jnp.float32)
        cache_blocks = cache_float[:, :LAT].reshape(block_count, LSEG, LAT)
        block_num = jnp.einsum('shbp,bpc->shbc', weights, cache_blocks)
        block_den = lax.optimization_barrier(jnp.sum(weights, -1))
        fresh_scores = jnp.einsum('shc,jc->shj', query_float, fresh_float) * score_scale
        fresh_scores = jnp.where(causal[:, None, :], fresh_scores, -1e+30)
        row_top = jnp.maximum(lax.optimization_barrier(jnp.max(block_top, -1)), lax.optimization_barrier(jnp.max(fresh_scores, -1)))
        factor = jnp.exp(block_top - row_top[..., None])
        fresh_weights = jnp.exp(fresh_scores - row_top[..., None]).astype(jnp.bfloat16).astype(jnp.float32)
        numerator = lax.optimization_barrier(jnp.sum(block_num * factor[..., None], 2)) + jnp.einsum('shj,jc->shc', fresh_weights, fresh_float[:, :LAT])
        denominator = lax.optimization_barrier(jnp.sum(block_den * factor, -1)) + lax.optimization_barrier(jnp.sum(fresh_weights, -1))
        mixed_heads = (numerator / denominator[..., None]).astype(jnp.bfloat16)
        return jnp.einsum('shc,hcv->shv', mixed_heads.astype(jnp.float32), value_float).astype(jnp.bfloat16)
    attended = lax.map(attend, (query_all, cache, new_latent, lengths))
    return (new_rows, attended)
```

```python
import math

import jax
import jax.numpy as jnp
from jax import lax
from jax.experimental import pallas as pl
from jax.experimental.pallas import tpu as pltpu
from jax.sharding import PartitionSpec as P

D = 7168
EPSILON = 1e-06
LAT = 512
ROW = 576
SEG = 512
SPAN = 384
REQS = 12
QPR = 16
X_REQS = 5
Z_REQS = 7
NX = X_REQS * QPR
NZ = Z_REQS * QPR
SPLIT = 48
PIECE = 96
SUB = 12
LOG2 = math.log2(math.e) / math.sqrt(192.0)
HIDE = -(2.0**99)
FLOOR = -(2.0**60)
F32 = jnp.float32
BF16 = jnp.bfloat16
VMEM_LIMIT = 48 * 1024 * 1024


def dot_nt(a, b):
    return lax.dot_general(a, b, (((1,), (1,)), ((), ())), preferred_element_type=F32)


def shift(value, dz, dx):
    pairs = [
        (z * 4 + x, (z + dz) % 8 * 4 + (x + dx) % 4) for z in range(8) for x in range(4)
    ]
    return lax.ppermute(value, "tp", pairs)


def flip_z(value, bit):
    return lax.ppermute(
        value, "tp", [(z * 4 + x, (z ^ bit) * 4 + x) for z in range(8) for x in range(4)]
    )


def params():
    return pltpu.CompilerParams(vmem_limit_bytes=VMEM_LIMIT)


def vmem():
    return pl.BlockSpec(memory_space=pltpu.VMEM)


def smem():
    return pl.BlockSpec(memory_space=pltpu.SMEM)


def two_terms(value):
    high = value.astype(BF16).astype(F32)
    return high, (value - high).astype(BF16).astype(F32)


def place_rows(rows, first=0):
    index = lax.broadcasted_iota(jnp.int32, (16, 128), 0)
    block = jnp.zeros((16, 128), F32)
    for k, row in enumerate(rows):
        block = jnp.where(index == first + k, row, block)
    return block


def eye_rows():
    a = lax.broadcasted_iota(jnp.int32, (128, 128), 0)
    b = lax.broadcasted_iota(jnp.int32, (128, 128), 1)
    return (a == b).astype(F32).astype(BF16)


def pick_rows(first):
    a = lax.broadcasted_iota(jnp.int32, (16, 128), 0)
    b = lax.broadcasted_iota(jnp.int32, (16, 128), 1)
    return ((a == b + first) & (b < 4)).astype(F32).astype(BF16)


def partial_softmax(query, keys, bias):
    scores = dot_nt(query, keys) + bias
    top = jnp.maximum(jnp.max(scores, -1, keepdims=True) * LOG2, FLOOR)
    high, low = two_terms(top)
    weights = jnp.exp2(scores * LOG2 - (high + low))
    total_high, total_low = two_terms(jnp.sum(weights, -1, keepdims=True))
    sums = jnp.dot(
        weights.astype(BF16), keys[:, :LAT], preferred_element_type=F32
    ).astype(BF16)
    lane = lax.broadcasted_iota(jnp.int32, (query.shape[0], 128), 1)
    stats = jnp.where(
        lane == 0,
        high,
        jnp.where(
            lane == 1,
            low,
            jnp.where(lane == 2, total_high, jnp.where(lane == 3, total_low, 0.0)),
        ),
    ).astype(BF16)
    return sums, stats


def project(x_index, hidden, in_gain, kv_weight):
    def kernel(x_ref, hidden_ref, gain_ref, weight_ref, *outs):
        lane = lax.broadcasted_iota(jnp.int32, (PIECE, 64), 1)
        for step, out in enumerate(outs):
            start = pl.multiple_of(lax.rem(x_ref[0] + step, 4) * PIECE, PIECE)
            rows = hidden_ref[pl.ds(start, PIECE), :].astype(F32)
            scaled = (rows * gain_ref[...].astype(F32)).astype(BF16)
            out[:, :ROW] = jnp.dot(
                scaled, weight_ref[...], preferred_element_type=F32
            ).astype(BF16)
            high, low = two_terms(jnp.sum(rows * rows, -1, keepdims=True))
            out[:, ROW:] = jnp.where(lane == 0, high, jnp.where(lane == 1, low, 0.0)).astype(
                BF16
            )

    return pl.pallas_call(
        kernel,
        out_shape=[jax.ShapeDtypeStruct((PIECE, 640), BF16)] * 4,
        in_specs=[smem(), vmem(), vmem(), vmem()],
        out_specs=[vmem()] * 4,
        compiler_params=params(),
        name="project",
    )(x_index, hidden, in_gain.reshape(1, -1), kv_weight)


def finish(z_index, mine, other, kv_gain, cosine, sine):
    def kernel(z_ref, mine_ref, other_ref, gain_ref, cos_ref, sin_ref, rows_ref, sub_ref):
        total = mine_ref[...].astype(F32) + other_ref[...].astype(F32)
        squares = total[:, ROW : ROW + 1] + total[:, ROW + 1 : ROW + 2]
        projected = total[:, :ROW] * lax.rsqrt(squares / D + EPSILON)
        latent = projected[:, :LAT]
        latent = (
            latent
            * lax.rsqrt(jnp.mean(latent * latent, -1, keepdims=True) + EPSILON)
            * gain_ref[...].astype(F32)
        )
        first = projected[:, LAT : LAT + 32]
        second = projected[:, LAT + 32 :]
        cos, sin = cos_ref[...], sin_ref[...]
        rows = jnp.concatenate(
            [latent, first * cos - second * sin, first * sin + second * cos], -1
        ).astype(BF16)
        rows_ref[...] = rows
        a = lax.broadcasted_iota(jnp.int32, (16, PIECE), 0)
        b = lax.broadcasted_iota(jnp.int32, (16, PIECE), 1)
        pick = ((b == a + z_ref[0] * SUB) & (a < SUB)).astype(F32).astype(BF16)
        sub_ref[...] = jnp.dot(pick, rows, preferred_element_type=F32).astype(BF16)

    return pl.pallas_call(
        kernel,
        out_shape=[
            jax.ShapeDtypeStruct((PIECE, ROW), BF16),
            jax.ShapeDtypeStruct((16, ROW), BF16),
        ],
        in_specs=[smem()] + [vmem()] * 5,
        out_specs=[vmem()] * 2,
        compiler_params=params(),
        name="finish",
    )(z_index, mine, other, kv_gain.reshape(1, -1), cosine, sine)


def absorb(order, q_nope, q_rope, key_absorb, new_latent):
    def kernel(order_ref, nope_ref, rope_ref, key_ref, new_ref, x_ref, z_ref, fx_ref, fz_ref):
        nope = jnp.concatenate([nope_ref[order_ref[i]] for i in range(REQS)], 0)
        rope = jnp.concatenate([rope_ref[order_ref[i]] for i in range(REQS)], 0)
        head = lax.broadcasted_iota(jnp.int32, (REQS * QPR, LAT), 0) % 4
        latent = jnp.zeros((REQS * QPR, LAT), F32)
        for h in range(4):
            part = jnp.dot(nope, key_ref[h], preferred_element_type=F32)
            latent = jnp.where(head == h, part, latent)
        query = jnp.concatenate([latent.astype(BF16), rope], -1)
        x_ref[...] = query[:NX]
        z_ref[...] = query[NX:]
        row = lax.broadcasted_iota(jnp.int32, (REQS * QPR, 4 * REQS), 0)
        column = lax.broadcasted_iota(jnp.int32, (REQS * QPR, 4 * REQS), 1)
        request = (row // QPR + order_ref[0]) % REQS
        seen = (column // 4 == request) & (column % 4 <= (row // 4) % 4)
        sums, stats = partial_softmax(query, new_ref[...], jnp.where(seen, 0.0, HIDE))
        for out, start, count in ((fx_ref, 0, NX), (fz_ref, NX, NZ)):
            out[:count, :] = sums[start : start + count]
            padded = jnp.concatenate(
                [stats[start : start + count], jnp.zeros((128 - count, 128), BF16)], 0
            )
            out[count:, :128] = dot_nt(pick_rows(0), padded).astype(BF16)
            out[count:, 128:] = jnp.zeros((16, 384), BF16)

    return pl.pallas_call(
        kernel,
        out_shape=[
            jax.ShapeDtypeStruct((NX, ROW), BF16),
            jax.ShapeDtypeStruct((NZ, ROW), BF16),
            jax.ShapeDtypeStruct((NX + 16, LAT), BF16),
            jax.ShapeDtypeStruct((NZ + 16, LAT), BF16),
        ],
        in_specs=[smem()] + [vmem()] * 4,
        out_specs=[vmem()] * 4,
        compiler_params=params(),
        name="absorb",
    )(order, q_nope, q_rope, key_absorb, new_latent)


def attend(order, cache, bias, queries, reqs, first, extra=None):
    counts = [q.shape[0] for q in queries]
    slots = sum(counts)
    rows = reqs * QPR
    n = len(queries)

    def kernel(order_ref, cache_ref, bias_ref, *refs):
        if extra is not None:
            extra_ref, extra_bias_ref, *refs = refs
        q_refs, out_refs, stat_ref = refs[:n], refs[n : 2 * n], refs[2 * n]
        i = pl.program_id(0)
        at = pl.multiple_of(i * QPR, QPR)

        @pl.when(i == 0)
        def _():
            stat_ref[...] = jnp.zeros_like(stat_ref)

        def work(keys, bias_row):
            query = jnp.concatenate(
                [
                    q[:, pl.ds(at, QPR), :].reshape(c * QPR, ROW)
                    for q, c in zip(q_refs, counts)
                ],
                0,
            )
            sums, stats = partial_softmax(query, keys, bias_row)
            stat_ref[:, pl.ds(at, QPR), :] = stats.reshape(slots, QPR, 128)
            k = 0
            for out, c in zip(out_refs, counts):
                for t in range(c):
                    out[pl.ds(pl.multiple_of(t * rows + at, QPR), QPR), :] = sums[
                        k * QPR : (k + 1) * QPR
                    ]
                    k += 1

        if extra is None:
            work(cache_ref[0], bias_ref[0])
        else:

            @pl.when(i < reqs - 1)
            def _():
                work(cache_ref[0], bias_ref[0])

            @pl.when(i == reqs - 1)
            def _():
                work(
                    jnp.concatenate([cache_ref[0], extra_ref[...]], 0),
                    jnp.concatenate([bias_ref[0], extra_bias_ref[...]], 1),
                )

        @pl.when(i == reqs - 1)
        def _():
            k = 0
            for out, c in zip(out_refs, counts):
                for group in range(4):
                    block = jnp.zeros((16, 128), F32)
                    for t in range(group, c, 4):
                        block += dot_nt(pick_rows(t // 4 * 4), stat_ref[k + t])
                    out[pl.ds(c * rows, 16), group * 128 : group * 128 + 128] = block.astype(
                        BF16
                    )
                k += c

    whole3 = lambda c: pl.BlockSpec((c, rows, ROW), lambda i, o: (0, 0, 0))
    extra_specs, extra_args = [], []
    if extra is not None:
        extra_specs = [
            pl.BlockSpec((128, ROW), lambda i, o: (0, 0)),
            pl.BlockSpec((1, 128), lambda i, o: (0, 0)),
        ]
        extra_args = list(extra)
    total = slots * QPR * reqs
    return pl.pallas_call(
        kernel,
        grid_spec=pltpu.PrefetchScalarGridSpec(
            num_scalar_prefetch=1,
            grid=(reqs,),
            in_specs=[
                pl.BlockSpec((1, SEG, ROW), lambda i, o: (o[first + i], 0, 0)),
                pl.BlockSpec((1, 1, SEG), lambda i, o: (o[first + i], 0, 0)),
            ]
            + extra_specs
            + [whole3(c) for c in counts],
            out_specs=[
                pl.BlockSpec((c * rows + 16, LAT), lambda i, o: (0, 0)) for c in counts
            ],
            scratch_shapes=[pltpu.VMEM((slots, 128, 128), BF16)],
        ),
        out_shape=[jax.ShapeDtypeStruct((c * rows + 16, LAT), BF16) for c in counts],
        compiler_params=params(),
        cost_estimate=pl.CostEstimate(
            flops=2 * total * SEG * (ROW + LAT),
            bytes_accessed=reqs * SEG * ROW * 2 + total * (ROW + LAT) * 2,
            transcendentals=total * SEG,
        ),
        name="attend",
    )(order, cache, bias, *extra_args, *queries)


def combine_slot(in_refs, shapes, sources, first, last):
    lane = lax.broadcasted_iota(jnp.int32, (1, 128), 1)
    tops, totals = [], []
    for which, slot in sources:
        count, low, high = shapes[which]
        base = count * (high - low)
        block = in_refs[which][base : base + 16, slot % 4 * 128 : slot % 4 * 128 + 128]
        block = block.astype(F32)
        g = slot // 4 * 4
        top = block[g : g + 1] + block[g + 1 : g + 2]
        total = block[g + 2 : g + 3] + block[g + 3 : g + 4]
        if low > first or high < last:
            inside = (lane >= low) & (lane < high)
            top = jnp.where(inside, top, FLOOR)
            total = jnp.where(inside, total, 0.0)
        tops.append(top)
        totals.append(total)
    top = tops[0]
    for other in tops[1:]:
        top = jnp.maximum(top, other)
    factors = [jnp.exp2(t - top) for t in tops]
    total = sum(f * t for f, t in zip(factors, totals))
    terms = [term for f in factors + [total] for term in two_terms(f)]
    columns = dot_nt(eye_rows(), place_rows(terms).astype(BF16))
    columns = [
        columns[:, 2 * k : 2 * k + 1] + columns[:, 2 * k + 1 : 2 * k + 2]
        for k in range(len(factors) + 1)
    ]
    cuts = {first, last}
    for which, _ in sources:
        cuts |= {max(first, shapes[which][1]), min(last, shapes[which][2])}
    cuts = sorted(cuts)
    segments = []
    for a, b in zip(cuts[:-1], cuts[1:]):
        value = None
        for (which, slot), column in zip(sources, columns):
            count, low, high = shapes[which]
            if low <= a and b <= high:
                at = slot * (high - low) + a - low
                part = in_refs[which][at : at + b - a, :].astype(F32) * column[a:b]
                value = part if value is None else value + part
        segments.append((a, b, value))
    return segments, top, total, columns[-1]


def merge(inputs, shapes, outs):
    def kernel(*refs):
        in_refs, out_refs = refs[: len(inputs)], refs[len(inputs) :]
        for out, (slots, first, last) in zip(out_refs, outs):
            rows = last - first
            base = len(slots) * rows
            blocks = [jnp.zeros((16, 128), F32) for _ in range(4)]
            for t, sources in enumerate(slots):
                segments, top, total, _ = combine_slot(in_refs, shapes, sources, first, last)
                for a, b, value in segments:
                    out[t * rows + a - first : t * rows + b - first, :] = value.astype(BF16)
                stats = [*two_terms(top), *two_terms(total)]
                blocks[t % 4] += place_rows(stats, t // 4 * 4)
            for group in range(4):
                out[base : base + 16, group * 128 : group * 128 + 128] = blocks[group].astype(
                    BF16
                )

    size = sum(v.size for v in inputs)
    return pl.pallas_call(
        kernel,
        out_shape=[
            jax.ShapeDtypeStruct((len(s) * (b - a) + 16, LAT), BF16) for s, a, b in outs
        ],
        in_specs=[vmem()] * len(inputs),
        out_specs=[vmem()] * len(outs),
        compiler_params=params(),
        cost_estimate=pl.CostEstimate(
            flops=4 * size, bytes_accessed=4 * size, transcendentals=0
        ),
        name="merge",
    )(*inputs)


def conclude(order, x_messages, z_messages, value_absorb):
    nx = len(x_messages)

    def kernel(order_ref, value_ref, *refs):
        out = refs[-1]
        parts = []
        for messages, rows in ((refs[:nx], NX), (refs[nx:-1], NZ)):
            shapes = [(1, 0, rows)] * len(messages)
            sources = [(k, 0) for k in range(len(messages))]
            segments, _, _, column = combine_slot(messages, shapes, sources, 0, rows)
            parts.append((segments[0][2] / column[:rows]).astype(BF16))
        mixed = jnp.concatenate(parts, 0)
        head = lax.broadcasted_iota(jnp.int32, (REQS * QPR, 128), 0) % 4
        result = jnp.zeros((REQS * QPR, 128), F32)
        for h in range(4):
            part = jnp.dot(mixed, value_ref[h], preferred_element_type=F32)
            result = jnp.where(head == h, part, result)
        result = result.astype(BF16)
        for i in range(REQS):
            out[order_ref[i]] = result[i * QPR : (i + 1) * QPR]

    return pl.pallas_call(
        kernel,
        out_shape=jax.ShapeDtypeStruct((REQS, QPR, 128), BF16),
        in_specs=[smem()] + [vmem()] * (1 + len(x_messages) + len(z_messages)),
        out_specs=vmem(),
        compiler_params=params(),
        name="conclude",
    )(order, value_absorb, *x_messages, *z_messages)


def per_device(
    hidden,
    in_gain,
    kv_weight,
    kv_gain,
    span_req,
    lengths,
    cache,
    q_nope,
    q_rope,
    new_latent,
    key_absorb,
    value_absorb,
):
    tp_index = lax.axis_index("tp")
    z_index, x_index = tp_index // 4, tp_index % 4
    group_index, dec_index = lax.axis_index("group"), lax.axis_index("dec")
    shard_index = group_index * 2 + dec_index
    table = jnp.arange(lengths.shape[0], dtype=jnp.int32)
    spans = jnp.arange(span_req.shape[0], dtype=jnp.int32)
    span_lengths = jnp.sum(
        jnp.where(span_req[:, None] == table[None, :], lengths[None, :], 0), -1
    )
    here = span_req // REQS == shard_index
    source = jnp.sum(jnp.where(here, spans, 0))
    place = jnp.sum(jnp.where(here, span_req % REQS, 0))
    span_start = jnp.sum(jnp.where(here, span_lengths, 0)) - SPAN
    order = (place + 1 + jnp.arange(REQS, dtype=jnp.int32)) % REQS

    positions = tp_index * SEG + jnp.arange(SEG, dtype=jnp.int32)
    my_lengths = lax.dynamic_slice_in_dim(lengths, shard_index * REQS, REQS)
    replaced = (positions >= span_start) & (positions < span_start + SPAN)
    is_span = jnp.arange(REQS) == place
    visible = (positions[None, :] < my_lengths[:, None]) & ~(
        is_span[:, None] & replaced[None, :]
    )
    bias = jnp.where(visible, 0.0, HIDE).astype(F32)[:, None, :]
    extra_bias = jnp.where(jnp.arange(128) < SUB, 0.0, HIDE).astype(F32)[None, :]

    pieces = project(x_index.reshape(1), hidden, in_gain, kv_weight)

    own_x, own_z, fresh_x, fresh_z = absorb(
        order,
        q_nope.reshape(REQS, QPR, 128),
        q_rope.reshape(REQS, QPR, 64),
        key_absorb,
        new_latent.reshape(REQS * 4, ROW),
    )

    bundle = jnp.stack([own_x, shift(own_x, 0, 1), shift(own_x, 0, -1), shift(own_x, 0, 2)])
    up = [bundle]
    down = [bundle]
    for _ in range(3):
        up.append(shift(up[-1], 1, 0))
        down.append(shift(down[-1], -1, 0))
    up.append(shift(up[-1][:2], 1, 0))
    down.append(shift(down[-1][2:], -1, 0))
    rise = [own_z]
    fall = [own_z]
    for _ in range(3):
        rise.append(shift(rise[-1], 1, 0))
        fall.append(shift(fall[-1], -1, 0))
    far = jnp.concatenate([shift(rise[3][:SPLIT], 1, 0), shift(fall[3][SPLIT:], -1, 0)], 0)
    column = jnp.stack([own_z, rise[1], fall[1], rise[2], fall[2], rise[3], fall[3], far])
    right = shift(column, 0, 1)
    left = shift(column, 0, -1)
    far_right = shift(right[:4], 0, 1)
    far_left = shift(left[4:], 0, -1)

    total = pieces[0].astype(F32)
    for step in range(1, 4):
        total = total + shift(pieces[step], 0, step).astype(F32)
    total = total.astype(BF16)
    for bit in (1, 2):
        total = (total.astype(F32) + flip_z(total, bit).astype(F32)).astype(BF16)
    span_me = jnp.sum(jnp.where(spans == shard_index, span_lengths, 0)) - SPAN
    row_positions = span_me + x_index * PIECE + jnp.arange(PIECE, dtype=jnp.int32)
    frequency = jnp.exp(jnp.arange(32, dtype=F32) * (-math.log(10000.0) / 32))
    angles = row_positions.astype(F32)[:, None] * frequency[None, :]
    rows, sub = finish(
        z_index.reshape(1), total, flip_z(total, 4), kv_gain, jnp.cos(angles), jnp.sin(angles)
    )
    near = jnp.stack([sub, lax.ppermute(sub, "dec", [(0, 1), (1, 0)])])
    around = [near] + [
        lax.ppermute(near, "group", [(g, (g + step) % 4) for g in range(4)])
        for step in range(1, 4)
    ]
    which = (group_index - source // 2) % 4 * 2 + (dec_index ^ (source % 2))
    extra = lax.dynamic_index_in_dim(jnp.concatenate(around, 0), which, 0, keepdims=False)
    extra = jnp.pad(extra, ((0, 112), (0, 0)))

    low = attend(order, cache, bias, [bundle, up[1], down[1], up[2], down[2]], X_REQS, 0)
    top = attend(order, cache, bias, [up[3], down[3], up[4], down[4]], X_REQS, 0)
    span_args = (extra, extra_bias)
    wide = attend(order, cache, bias, [column, right, left], Z_REQS, X_REQS, span_args)
    ends = attend(order, cache, bias, [far_right, far_left], Z_REQS, X_REQS, span_args)

    four = (4, 0, NX)
    two = (2, 0, NX)
    one = (1, 0, NX)
    from_up = shift(top[2], -1, 0)
    from_down = shift(top[3], 1, 0)
    up_sum, down_sum = merge(
        [top[0], top[1], from_up, from_down],
        [four, four, two, two],
        [
            ([[(0, 0), (2, 0)], [(0, 1), (2, 1)], [(0, 2)], [(0, 3)]], 0, NX),
            ([[(1, 0)], [(1, 1)], [(1, 2), (3, 0)], [(1, 3), (3, 1)]], 0, NX),
        ],
    )
    for level in (2, 1):
        from_up = shift(up_sum, -1, 0)
        from_down = shift(down_sum, 1, 0)
        up_sum, down_sum = merge(
            [low[2 * level - 1], low[2 * level], from_up, from_down],
            [four] * 4,
            [
                ([[(0, t), (2, t)] for t in range(4)], 0, NX),
                ([[(1, t), (3, t)] for t in range(4)], 0, NX),
            ],
        )
    from_up = shift(up_sum, -1, 0)
    from_down = shift(down_sum, 1, 0)
    own = merge(
        [low[0], from_up, from_down],
        [four] * 3,
        [([[(0, t), (1, t), (2, t)]], 0, NX) for t in range(4)],
    )
    x_messages = [
        own[0],
        shift(own[1], 0, -1),
        shift(own[2], 0, 1),
        shift(own[3], 0, 2),
        fresh_x,
    ]

    eight = (8, 0, NZ)
    from_right = shift(ends[0], 0, -1)
    from_left = shift(ends[1], 0, 1)
    right_sum, left_sum = merge(
        [wide[1], wide[2], from_right, from_left],
        [eight, eight, (4, 0, NZ), (4, 0, NZ)],
        [
            ([[(0, t), (2, t)] for t in range(4)] + [[(0, t)] for t in range(4, 8)], 0, NZ),
            ([[(1, t)] for t in range(4)] + [[(1, t), (3, t - 4)] for t in range(4, 8)], 0, NZ),
        ],
    )
    from_right = shift(right_sum, 0, -1)
    from_left = shift(left_sum, 0, 1)
    every = lambda t: [[(0, t), (1, t), (2, t)]]
    mine, rise1, fall1, rise2, fall2, rise3, fall3, far_up, far_down = merge(
        [wide[0], from_right, from_left],
        [eight] * 3,
        [(every(t), 0, NZ) for t in range(7)] + [(every(7), 0, SPLIT), (every(7), SPLIT, NZ)],
    )
    unit = (1, 0, NZ)
    pair = [([[(0, 0), (2, 0)]], 0, NZ), ([[(1, 0), (3, 0)]], 0, NZ)]
    rise_sum, fall_sum = merge(
        [rise3, fall3, shift(far_up, -1, 0), shift(far_down, 1, 0)],
        [unit, unit, (1, 0, SPLIT), (1, SPLIT, NZ)],
        pair,
    )
    for rise_own, fall_own in ((rise2, fall2), (rise1, fall1)):
        rise_sum, fall_sum = merge(
            [rise_own, fall_own, shift(rise_sum, -1, 0), shift(fall_sum, 1, 0)],
            [unit] * 4,
            pair,
        )
    z_messages = [mine, shift(rise_sum, -1, 0), shift(fall_sum, 1, 0), fresh_z]

    attended = conclude(order, x_messages, z_messages, value_absorb)

    ring = [rows] + [shift(rows, 0, -step) for step in range(1, 4)]
    ring = jnp.concatenate(ring + ring, 0)
    new_rows = lax.dynamic_slice_in_dim(ring, (4 - x_index) % 4 * PIECE, SPAN)
    return (new_rows, attended.reshape(REQS, 4, 4, 128))


def solution(mesh):
    return jax.shard_map(
        per_device,
        mesh=mesh,
        in_specs=(
            P(("group", "dec"), "tp"),
            P("tp"),
            P("tp", None),
            P(),
            P(),
            P(),
            P(("group", "dec"), "tp", None),
            P(("group", "dec"), None, "tp", None),
            P(("group", "dec"), None, "tp", None),
            P(("group", "dec"), None, None),
            P("tp", None, None),
            P("tp", None, None),
        ),
        out_specs=(P(("group", "dec"), None), P(("group", "dec"), None, "tp", None)),
        check_vma=False,
    )
```

```python
import math

import jax
import jax.numpy as jnp
from jax import lax
from jax.experimental import pallas as pl
from jax.experimental.pallas import tpu as pltpu
from jax.sharding import PartitionSpec as P

D = 7168
EPSILON = 1e-06
LAT = 512
ROW = 576
SEG = 512
SPAN = 384
REQS = 12
QPR = 16
HALF = 6
NQ = HALF * QPR
MSG = NQ + 16
SPLIT = 48
PIECE = 96
SUB = 12
LOG2 = math.log2(math.e) / math.sqrt(192.0)
HIDE = -(2.0**99)
FLOOR = -(2.0**60)
F32 = jnp.float32
BF16 = jnp.bfloat16


def dot_nt(a, b):
    return lax.dot_general(a, b, (((1,), (1,)), ((), ())), preferred_element_type=F32)


def shift(value, dz, dx):
    pairs = [
        (z * 4 + x, (z + dz) % 8 * 4 + (x + dx) % 4) for z in range(8) for x in range(4)
    ]
    return lax.ppermute(value, "tp", pairs)


def flip_z(value, bit):
    return lax.ppermute(
        value, "tp", [(z * 4 + x, (z ^ bit) * 4 + x) for z in range(8) for x in range(4)]
    )


def params(mib):
    return pltpu.CompilerParams(vmem_limit_bytes=mib * 1024 * 1024)


def vmem():
    return pl.BlockSpec(memory_space=pltpu.VMEM)


def smem():
    return pl.BlockSpec(memory_space=pltpu.SMEM)


def two_terms(value):
    high = value.astype(BF16).astype(F32)
    return high, (value - high).astype(BF16).astype(F32)


def place_rows(rows, first=0):
    index = lax.broadcasted_iota(jnp.int32, (16, 128), 0)
    block = jnp.zeros((16, 128), F32)
    for k, row in enumerate(rows):
        block = jnp.where(index == first + k, row, block)
    return block


def eye_rows():
    a = lax.broadcasted_iota(jnp.int32, (128, 128), 0)
    b = lax.broadcasted_iota(jnp.int32, (128, 128), 1)
    return (a == b).astype(F32).astype(BF16)


def pick_rows(first):
    a = lax.broadcasted_iota(jnp.int32, (16, 128), 0)
    b = lax.broadcasted_iota(jnp.int32, (16, 128), 1)
    return ((a == b + first) & (b < 4)).astype(F32).astype(BF16)


def soften(scores):
    top = jnp.maximum(jnp.max(scores, -1, keepdims=True) * LOG2, FLOOR)
    high, low = two_terms(top)
    weights = jnp.exp2(scores * LOG2 - (high + low))
    total_high, total_low = two_terms(jnp.sum(weights, -1, keepdims=True))
    lane = lax.broadcasted_iota(jnp.int32, (scores.shape[0], 128), 1)
    stats = jnp.where(
        lane == 0,
        high,
        jnp.where(
            lane == 1,
            low,
            jnp.where(lane == 2, total_high, jnp.where(lane == 3, total_low, 0.0)),
        ),
    ).astype(BF16)
    return weights.astype(BF16), stats


def work_order(span_ref, shard):
    place = jnp.int32(0)
    for g in range(8):
        request = span_ref[g]
        place = jnp.where(lax.div(request, REQS) == shard, lax.rem(request, REQS), place)
    return [lax.rem(place + 1 + i, REQS) for i in range(REQS)]


def prepare(place, span_req, hidden_t, in_gain, kv_weight, q_nope, q_rope, key_absorb):
    def kernel(
        place_ref, span_ref, hidden_ref, gain_ref, weight_ref, nope_ref, rope_ref, key_ref,
        x_ref, z_ref, own_ref, *rest,
    ):
        sends, scratch = rest[:3], rest[3]
        order = work_order(span_ref, place_ref[1])
        nope = jnp.concatenate([nope_ref[i] for i in order], 0)
        head = lax.broadcasted_iota(jnp.int32, (REQS * QPR, LAT), 0) % 4
        latent = jnp.zeros((REQS * QPR, LAT), F32)
        for h in range(4):
            part = jnp.dot(nope, key_ref[h], preferred_element_type=F32)
            latent = jnp.where(head == h, part, latent)
        latent = latent.astype(BF16)
        for out, base in ((x_ref, 0), (z_ref, HALF)):
            out[:NQ, :] = latent[base * QPR : base * QPR + NQ]
            for i in range(HALF):
                out[NQ:, 64 * i : 64 * i + 64] = rope_ref[order[base + i]]
            out[NQ:, 64 * HALF :] = jnp.zeros((16, LAT - 64 * HALF), BF16)

        a = lax.broadcasted_iota(jnp.int32, (224, 224), 0)
        b = lax.broadcasted_iota(jnp.int32, (224, 224), 1)
        eye = (a == b).astype(F32).astype(BF16)
        gain = dot_nt(eye, jnp.broadcast_to(gain_ref[...], (16, 224)))[:, :1]
        rows = hidden_ref[...].astype(F32)
        over_rows = (((0,), (0,)), ((), ()))
        scratch[:, :ROW] = lax.dot_general(
            (rows * gain).astype(BF16), weight_ref[...], over_rows, preferred_element_type=F32
        ).astype(BF16)
        ones = jnp.ones((224, 128), BF16)
        squares = sum(
            lax.dot_general(term.astype(BF16), ones, over_rows, preferred_element_type=F32)
            for term in two_terms(rows * rows)
        )[:, :64]
        lane = lax.broadcasted_iota(jnp.int32, (SPAN, 64), 1)
        high, low = two_terms(squares)
        scratch[:, ROW:] = jnp.where(lane == 0, high, jnp.where(lane == 1, low, 0.0)).astype(BF16)
        for step, (out, first) in enumerate([(own_ref, 0)] + [(o, MSG) for o in sends]):
            start = pl.multiple_of(lax.rem(place_ref[0] + step, 4) * PIECE, PIECE)
            piece = scratch[pl.ds(start, PIECE), :]
            out[first : first + PIECE, :] = piece[:, :LAT]
            for j in range(3):
                out[first + PIECE : first + PIECE + 32, 128 * j : 128 * j + 128] = piece[
                    32 * j : 32 * j + 32, LAT:
                ]
            out[first + PIECE : first + PIECE + 32, 384:] = jnp.zeros((32, 128), BF16)
            if step:
                out[:MSG, :] = x_ref[...]

    shard = jax.ShapeDtypeStruct((MSG, LAT), BF16)
    return pl.pallas_call(
        kernel,
        out_shape=[shard, shard, jax.ShapeDtypeStruct((PIECE + 32, LAT), BF16)]
        + [jax.ShapeDtypeStruct((MSG + PIECE + 32, LAT), BF16)] * 3,
        in_specs=[smem()] * 2 + [vmem()] * 6,
        out_specs=[vmem()] * 6,
        scratch_shapes=[pltpu.VMEM((SPAN, 640), BF16)],
        compiler_params=params(12),
        name="prepare",
    )(
        place, span_req, hidden_t, in_gain.reshape(1, -1), kv_weight, q_nope, q_rope, key_absorb
    )


def finish(z_index, mine, other, kv_gain, cosine, sine):
    def kernel(z_ref, mine_ref, other_ref, gain_ref, cos_ref, sin_ref, rows_ref, sub_ref):
        total = mine_ref[...].astype(F32) + other_ref[...].astype(F32)
        tail = jnp.concatenate(
            [total[PIECE:, 128 * j : 128 * j + 128] for j in range(3)], 0
        )
        scale = lax.rsqrt((tail[:, 64:65] + tail[:, 65:66]) / D + EPSILON)
        latent = total[:PIECE] * scale
        latent = (
            latent
            * lax.rsqrt(jnp.mean(latent * latent, -1, keepdims=True) + EPSILON)
            * gain_ref[...].astype(F32)
        )
        first = tail[:, :32] * scale
        second = tail[:, 32:64] * scale
        cos, sin = cos_ref[...], sin_ref[...]
        rope = jnp.concatenate([first * cos - second * sin, first * sin + second * cos], -1)
        rows = jnp.concatenate([latent, rope], -1).astype(BF16)
        rows_ref[:PIECE, :] = rows[:, :LAT]
        for j in range(6):
            rows_ref[PIECE:, 64 * j : 64 * j + 64] = rows[16 * j : 16 * j + 16, LAT:]
        rows_ref[PIECE:, 384:] = jnp.zeros((16, 128), BF16)
        a = lax.broadcasted_iota(jnp.int32, (16, PIECE), 0)
        b = lax.broadcasted_iota(jnp.int32, (16, PIECE), 1)
        pick = ((b == a + z_ref[0] * SUB) & (a < SUB)).astype(F32).astype(BF16)
        sub_ref[...] = jnp.dot(pick, rows, preferred_element_type=F32).astype(BF16)

    return pl.pallas_call(
        kernel,
        out_shape=[
            jax.ShapeDtypeStruct((MSG, LAT), BF16),
            jax.ShapeDtypeStruct((16, ROW), BF16),
        ],
        in_specs=[smem()] + [vmem()] * 5,
        out_specs=[vmem()] * 2,
        compiler_params=params(8),
        name="finish",
    )(z_index, mine, other, kv_gain.reshape(1, -1), cosine, sine)


def unpack(x_index, own, received):
    def kernel(x_ref, *refs):
        out = refs[-1]
        for step, ref in enumerate(refs[:-1]):
            base = MSG if step else 0
            start = pl.multiple_of(lax.rem(x_ref[0] + step, 4) * PIECE, PIECE)
            out[pl.ds(start, PIECE), :LAT] = ref[base : base + PIECE, :]
            out[pl.ds(start, PIECE), LAT:] = jnp.concatenate(
                [ref[base + PIECE : base + MSG, 64 * j : 64 * j + 64] for j in range(6)], 0
            )

    return pl.pallas_call(
        kernel,
        out_shape=jax.ShapeDtypeStruct((SPAN, ROW), BF16),
        in_specs=[smem()] + [vmem()] * 4,
        out_specs=vmem(),
        compiler_params=params(8),
        name="unpack",
    )(x_index, own, *received)


def fresh(place, span_req, own_x, own_z, q_rope, new_latent):
    def kernel(place_ref, span_ref, x_ref, z_ref, rope_ref, new_ref, fx_ref, fz_ref):
        order = work_order(span_ref, place_ref[1])
        rope = jnp.concatenate([rope_ref[i] for i in order], 0)
        latent = jnp.concatenate([x_ref[:NQ, :], z_ref[:NQ, :]], 0)
        row = lax.broadcasted_iota(jnp.int32, (REQS * QPR, 4 * REQS), 0)
        column = lax.broadcasted_iota(jnp.int32, (REQS * QPR, 4 * REQS), 1)
        request = lax.rem(row // QPR + order[0], REQS)
        seen = (column // 4 == request) & (column % 4 <= (row // 4) % 4)
        scores = dot_nt(latent, new_ref[:, :LAT]) + dot_nt(rope, new_ref[:, LAT:])
        weights, stats = soften(scores + jnp.where(seen, 0.0, HIDE))
        sums = jnp.dot(weights, new_ref[:, :LAT], preferred_element_type=F32).astype(BF16)
        for out, start in ((fx_ref, 0), (fz_ref, NQ)):
            out[:NQ, :] = sums[start : start + NQ]
            padded = jnp.concatenate(
                [stats[start : start + NQ], jnp.zeros((128 - NQ, 128), BF16)], 0
            )
            out[NQ:, :128] = dot_nt(pick_rows(0), padded).astype(BF16)
            out[NQ:, 128:] = jnp.zeros((16, 384), BF16)

    return pl.pallas_call(
        kernel,
        out_shape=[jax.ShapeDtypeStruct((MSG, LAT), BF16)] * 2,
        in_specs=[smem()] * 2 + [vmem()] * 4,
        out_specs=[vmem()] * 2,
        compiler_params=params(8),
        name="fresh",
    )(place, span_req, own_x, own_z, q_rope, new_latent)


def attend(order, cache_t, bias, queries, first, extra=None):
    counts = [q.shape[0] for q in queries]
    slots = sum(counts)
    n = len(queries)
    steps = HALF // 2

    def kernel(order_ref, *refs):
        cache_refs, bias_refs, refs = refs[:2], refs[2:4], refs[4:]
        if extra is not None:
            extra_ref, extra_bias_ref, *refs = refs
        q_refs, out_refs, stat_ref = refs[:n], refs[n : 2 * n], refs[2 * n]
        i = pl.program_id(0)

        @pl.when(i == 0)
        def _():
            stat_ref[...] = jnp.zeros_like(stat_ref)

        lanes = pl.ds(pl.multiple_of(i * 128, 128), 128)
        rope = jnp.concatenate(
            [q[:, NQ:, lanes].reshape(c * QPR, 128) for q, c in zip(q_refs, counts)], 0
        )
        for side in range(2):
            at = pl.multiple_of(i * (2 * QPR) + side * QPR, QPR)
            keys = cache_refs[side][0]
            bias_row = bias_refs[side][0]
            if extra is not None and side == 1:
                keys = jnp.concatenate([keys, extra_ref[...]], 1)
                hidden_row = jnp.where(i == steps - 1, extra_bias_ref[...], HIDE)
                bias_row = jnp.concatenate([bias_row, hidden_row], 1)
            latent = jnp.concatenate(
                [
                    q[:, pl.ds(at, QPR), :].reshape(c * QPR, LAT)
                    for q, c in zip(q_refs, counts)
                ],
                0,
            )
            turned = [keys[LAT:], jnp.zeros((64, keys.shape[1]), BF16)]
            turned = jnp.concatenate(turned if side == 0 else turned[::-1], 0)
            scores = jnp.dot(latent, keys[:LAT], preferred_element_type=F32)
            scores = scores + jnp.dot(rope, turned, preferred_element_type=F32)
            weights, stats = soften(scores + bias_row)
            sums = dot_nt(weights, keys[:LAT]).astype(BF16)
            stat_ref[:, pl.ds(at, QPR), :] = stats.reshape(slots, QPR, 128)
            k = 0
            for out, c in zip(out_refs, counts):
                for t in range(c):
                    out[pl.ds(pl.multiple_of(t * NQ + at, QPR), QPR), :] = sums[
                        k * QPR : (k + 1) * QPR
                    ]
                    k += 1

        @pl.when(i == steps - 1)
        def _():
            k = 0
            for out, c in zip(out_refs, counts):
                for group in range(4):
                    block = jnp.zeros((16, 128), F32)
                    for t in range(group, c, 4):
                        block += dot_nt(pick_rows(t // 4 * 4), stat_ref[k + t])
                    out[pl.ds(c * NQ, 16), group * 128 : group * 128 + 128] = block.astype(BF16)
                k += c

    def at_side(shape, side):
        return pl.BlockSpec(shape, lambda i, o: (o[first + 2 * i + side], 0, 0))

    extra_args = list(extra) if extra is not None else []
    total = slots * QPR * HALF
    return pl.pallas_call(
        kernel,
        grid_spec=pltpu.PrefetchScalarGridSpec(
            num_scalar_prefetch=1,
            grid=(steps,),
            in_specs=[at_side((1, ROW, SEG), side) for side in range(2)]
            + [at_side((1, 1, SEG), side) for side in range(2)]
            + [vmem()] * (len(extra_args) + n),
            out_specs=[vmem()] * n,
            scratch_shapes=[pltpu.VMEM((slots, 128, 128), BF16)],
        ),
        out_shape=[jax.ShapeDtypeStruct((c * NQ + 16, LAT), BF16) for c in counts],
        compiler_params=params(16),
        cost_estimate=pl.CostEstimate(
            flops=2 * total * SEG * (ROW + LAT),
            bytes_accessed=HALF * SEG * ROW * 2 + total * (ROW + LAT) * 2,
            transcendentals=total * SEG,
        ),
        name="attend",
    )(order, cache_t, cache_t, bias, bias, *extra_args, *queries)


def combine_slot(in_refs, shapes, sources, first, last):
    lane = lax.broadcasted_iota(jnp.int32, (1, 128), 1)
    tops, totals = [], []
    for which, slot in sources:
        count, low, high = shapes[which]
        base = count * (high - low)
        block = in_refs[which][base : base + 16, slot % 4 * 128 : slot % 4 * 128 + 128]
        block = block.astype(F32)
        g = slot // 4 * 4
        top = block[g : g + 1] + block[g + 1 : g + 2]
        total = block[g + 2 : g + 3] + block[g + 3 : g + 4]
        if low > first or high < last:
            inside = (lane >= low) & (lane < high)
            top = jnp.where(inside, top, FLOOR)
            total = jnp.where(inside, total, 0.0)
        tops.append(top)
        totals.append(total)
    top = tops[0]
    for other in tops[1:]:
        top = jnp.maximum(top, other)
    factors = [jnp.exp2(t - top) for t in tops]
    total = sum(f * t for f, t in zip(factors, totals))
    terms = [term for f in factors + [total] for term in two_terms(f)]
    columns = dot_nt(eye_rows(), place_rows(terms).astype(BF16))
    columns = [
        columns[:, 2 * k : 2 * k + 1] + columns[:, 2 * k + 1 : 2 * k + 2]
        for k in range(len(factors) + 1)
    ]
    cuts = {first, last}
    for which, _ in sources:
        cuts |= {max(first, shapes[which][1]), min(last, shapes[which][2])}
    cuts = sorted(cuts)
    segments = []
    for a, b in zip(cuts[:-1], cuts[1:]):
        value = None
        for (which, slot), column in zip(sources, columns):
            count, low, high = shapes[which]
            if low <= a and b <= high:
                at = slot * (high - low) + a - low
                part = in_refs[which][at : at + b - a, :].astype(F32) * column[a:b]
                value = part if value is None else value + part
        segments.append((a, b, value))
    return segments, top, total, columns[-1]


def merge(inputs, shapes, outs, append=None):
    extra = [] if append is None else [append]

    def kernel(*refs):
        in_refs = refs[: len(inputs)]
        out_refs = refs[len(inputs) + len(extra) :]
        for out, (slots, first, last, *appended) in zip(out_refs, outs):
            rows = last - first
            base = len(slots) * rows
            blocks = [jnp.zeros((16, 128), F32) for _ in range(4)]
            for t, sources in enumerate(slots):
                segments, top, total, _ = combine_slot(in_refs, shapes, sources, first, last)
                for a, b, value in segments:
                    out[t * rows + a - first : t * rows + b - first, :] = value.astype(BF16)
                stats = [*two_terms(top), *two_terms(total)]
                blocks[t % 4] += place_rows(stats, t // 4 * 4)
            for group in range(4):
                out[base : base + 16, group * 128 : group * 128 + 128] = blocks[group].astype(
                    BF16
                )
            if appended:
                out[base + 16 :, :] = refs[len(inputs)][...]

    size = sum(v.size for v in inputs)
    return pl.pallas_call(
        kernel,
        out_shape=[
            jax.ShapeDtypeStruct(
                (len(s) * (b - a) + 16 + (append.shape[0] if more else 0), LAT), BF16
            )
            for s, a, b, *more in outs
        ],
        in_specs=[vmem()] * (len(inputs) + len(extra)),
        out_specs=[vmem()] * len(outs),
        compiler_params=params(8),
        cost_estimate=pl.CostEstimate(
            flops=4 * size, bytes_accessed=4 * size, transcendentals=0
        ),
        name="merge",
    )(*inputs, *extra)


def conclude(order, x_messages, z_messages, value_absorb):
    nx = len(x_messages)

    def kernel(order_ref, value_ref, *refs):
        out = refs[-1]
        parts = []
        for messages in (refs[:nx], refs[nx:-1]):
            shapes = [(1, 0, NQ)] * len(messages)
            sources = [(k, 0) for k in range(len(messages))]
            segments, _, _, column = combine_slot(messages, shapes, sources, 0, NQ)
            parts.append((segments[0][2] / column[:NQ]).astype(BF16))
        mixed = jnp.concatenate(parts, 0)
        head = lax.broadcasted_iota(jnp.int32, (REQS * QPR, 128), 0) % 4
        result = jnp.zeros((REQS * QPR, 128), F32)
        for h in range(4):
            part = jnp.dot(mixed, value_ref[h], preferred_element_type=F32)
            result = jnp.where(head == h, part, result)
        result = result.astype(BF16)
        for i in range(REQS):
            out[order_ref[i]] = result[i * QPR : (i + 1) * QPR]

    return pl.pallas_call(
        kernel,
        out_shape=jax.ShapeDtypeStruct((REQS, QPR, 128), BF16),
        in_specs=[smem()] + [vmem()] * (1 + len(x_messages) + len(z_messages)),
        out_specs=vmem(),
        compiler_params=params(8),
        name="conclude",
    )(order, value_absorb, *x_messages, *z_messages)


def per_device(
    hidden,
    in_gain,
    kv_weight,
    kv_gain,
    span_req,
    lengths,
    cache,
    q_nope,
    q_rope,
    new_latent,
    key_absorb,
    value_absorb,
):
    tp_index = lax.axis_index("tp")
    z_index, x_index = tp_index // 4, tp_index % 4
    group_index, dec_index = lax.axis_index("group"), lax.axis_index("dec")
    shard_index = group_index * 2 + dec_index
    place_args = (jnp.stack([x_index, shard_index]).astype(jnp.int32), span_req)
    rope = q_rope.reshape(REQS, QPR, 64)
    own_x, own_z, piece, send1, send2, send3 = prepare(
        *place_args,
        hidden.T,
        in_gain,
        kv_weight,
        q_nope.reshape(REQS, QPR, 128),
        rope,
        key_absorb,
    )

    from_left = shift(send1, 0, 1)
    from_right = shift(send3, 0, -1)
    from_across = shift(send2, 0, 2)
    bundle = jnp.stack([own_x, from_left[:MSG], from_right[:MSG], from_across[:MSG]])
    total = piece.astype(F32)
    for received in (from_left, from_right, from_across):
        total = total + received[MSG:].astype(F32)
    total = total.astype(BF16)
    rise = [own_z]
    fall = [own_z]
    for _ in range(3):
        rise.append(shift(rise[-1], 1, 0))
        fall.append(shift(fall[-1], -1, 0))
    far = jnp.concatenate([shift(rise[3][:SPLIT], 1, 0), shift(fall[3][SPLIT:], -1, 0)], 0)
    column = jnp.stack([own_z, rise[1], fall[1], rise[2], fall[2], rise[3], fall[3], far])
    for bit in (1, 2):
        total = (total.astype(F32) + flip_z(total, bit).astype(F32)).astype(BF16)
    total_other = flip_z(total, 4)
    bundle, column, total, total_other = lax.optimization_barrier(
        (bundle, column, total, total_other)
    )
    up = [bundle]
    down = [bundle]
    for _ in range(3):
        up.append(shift(up[-1], 1, 0))
        down.append(shift(down[-1], -1, 0))
    up.append(shift(up[-1][:2], 1, 0))
    down.append(shift(down[-1][2:], -1, 0))
    right = shift(column, 0, 1)
    left = shift(column, 0, -1)
    far_right = shift(right[:4], 0, 1)
    far_left = shift(left[4:], 0, -1)

    table = jnp.arange(lengths.shape[0], dtype=jnp.int32)
    spans = jnp.arange(span_req.shape[0], dtype=jnp.int32)
    span_lengths = jnp.sum(
        jnp.where(span_req[:, None] == table[None, :], lengths[None, :], 0), -1
    )
    here = span_req // REQS == shard_index
    source = jnp.sum(jnp.where(here, spans, 0))
    place = jnp.sum(jnp.where(here, span_req % REQS, 0))
    span_start = jnp.sum(jnp.where(here, span_lengths, 0)) - SPAN
    order = (place + 1 + jnp.arange(REQS, dtype=jnp.int32)) % REQS
    positions = tp_index * SEG + jnp.arange(SEG, dtype=jnp.int32)
    my_lengths = lax.dynamic_slice_in_dim(lengths, shard_index * REQS, REQS)
    replaced = (positions >= span_start) & (positions < span_start + SPAN)
    is_span = jnp.arange(REQS) == place
    visible = (positions[None, :] < my_lengths[:, None]) & ~(
        is_span[:, None] & replaced[None, :]
    )
    bias = jnp.where(visible, 0.0, HIDE).astype(F32)[:, None, :]
    extra_bias = jnp.where(jnp.arange(128) < SUB, 0.0, HIDE).astype(F32)[None, :]

    span_me = jnp.sum(jnp.where(spans == shard_index, span_lengths, 0)) - SPAN
    row_positions = span_me + x_index * PIECE + jnp.arange(PIECE, dtype=jnp.int32)
    frequency = jnp.exp(jnp.arange(32, dtype=F32) * (-math.log(10000.0) / 32))
    angles = row_positions.astype(F32)[:, None] * frequency[None, :]
    rows, sub = finish(
        z_index.reshape(1), total, total_other, kv_gain, jnp.cos(angles), jnp.sin(angles)
    )
    near = jnp.stack([sub, lax.ppermute(sub, "dec", [(0, 1), (1, 0)])])
    around = [near] + [
        lax.ppermute(near, "group", [(g, (g + step) % 4) for g in range(4)])
        for step in range(1, 4)
    ]
    which = (group_index - source // 2) % 4 * 2 + (dec_index ^ (source % 2))
    extra = lax.dynamic_index_in_dim(jnp.concatenate(around, 0), which, 0, keepdims=False)
    extra = jnp.pad(extra, ((0, 112), (0, 0))).T

    fresh_x, fresh_z = fresh(*place_args, own_x, own_z, rope, new_latent.reshape(REQS * 4, ROW))

    cache_t = jnp.swapaxes(cache, 1, 2)
    span_args = (extra, extra_bias)
    low = attend(order, cache_t, bias, [bundle, up[1], down[1], up[2], down[2]], 0)
    wide = attend(order, cache_t, bias, [column, right, left], HALF, span_args)
    top = attend(order, cache_t, bias, [up[3], down[3], up[4], down[4]], 0)
    ends = attend(order, cache_t, bias, [far_right, far_left], HALF, span_args)

    four = (4, 0, NQ)
    two = (2, 0, NQ)
    from_up = shift(top[2], -1, 0)
    from_down = shift(top[3], 1, 0)
    up_sum, down_sum = merge(
        [top[0], top[1], from_up, from_down],
        [four, four, two, two],
        [
            ([[(0, 0), (2, 0)], [(0, 1), (2, 1)], [(0, 2)], [(0, 3)]], 0, NQ),
            ([[(1, 0)], [(1, 1)], [(1, 2), (3, 0)], [(1, 3), (3, 1)]], 0, NQ),
        ],
    )
    for level in (2, 1):
        from_up = shift(up_sum, -1, 0)
        from_down = shift(down_sum, 1, 0)
        up_sum, down_sum = merge(
            [low[2 * level - 1], low[2 * level], from_up, from_down],
            [four] * 4,
            [
                ([[(0, t), (2, t)] for t in range(4)], 0, NQ),
                ([[(1, t), (3, t)] for t in range(4)], 0, NQ),
            ],
        )
    from_up = shift(up_sum, -1, 0)
    from_down = shift(down_sum, 1, 0)
    own = merge(
        [low[0], from_up, from_down],
        [four] * 3,
        [
            ([[(0, t), (1, t), (2, t)]], 0, NQ, *((True,) if t else ()))
            for t in range(4)
        ],
        rows,
    )
    x_received = [shift(own[2], 0, 1), shift(own[1], 0, -1), shift(own[3], 0, 2)]

    eight = (8, 0, NQ)
    from_right = shift(ends[0], 0, -1)
    from_left = shift(ends[1], 0, 1)
    right_sum, left_sum = merge(
        [wide[1], wide[2], from_right, from_left],
        [eight, eight, four, four],
        [
            ([[(0, t), (2, t)] for t in range(4)] + [[(0, t)] for t in range(4, 8)], 0, NQ),
            ([[(1, t)] for t in range(4)] + [[(1, t), (3, t - 4)] for t in range(4, 8)], 0, NQ),
        ],
    )
    from_right = shift(right_sum, 0, -1)
    from_left = shift(left_sum, 0, 1)
    every = lambda t: [[(0, t), (1, t), (2, t)]]
    mine, rise1, fall1, rise2, fall2, rise3, fall3, far_up, far_down = merge(
        [wide[0], from_right, from_left],
        [eight] * 3,
        [(every(t), 0, NQ) for t in range(7)] + [(every(7), 0, SPLIT), (every(7), SPLIT, NQ)],
    )
    unit = (1, 0, NQ)
    pair = [([[(0, 0), (2, 0)]], 0, NQ), ([[(1, 0), (3, 0)]], 0, NQ)]
    rise_sum, fall_sum = merge(
        [rise3, fall3, shift(far_up, -1, 0), shift(far_down, 1, 0)],
        [unit, unit, (1, 0, SPLIT), (1, SPLIT, NQ)],
        pair,
    )
    for rise_own, fall_own in ((rise2, fall2), (rise1, fall1)):
        rise_sum, fall_sum = merge(
            [rise_own, fall_own, shift(rise_sum, -1, 0), shift(fall_sum, 1, 0)],
            [unit] * 4,
            pair,
        )
    z_messages = [mine, shift(rise_sum, -1, 0), shift(fall_sum, 1, 0), fresh_z]

    new_rows = unpack(
        x_index.reshape(1), rows, [x_received[1], x_received[2], x_received[0]]
    )
    attended = conclude(order, [own[0], *x_received, fresh_x], z_messages, value_absorb)
    return (new_rows, attended.reshape(REQS, 4, 4, 128))


def solution(mesh):
    return jax.shard_map(
        per_device,
        mesh=mesh,
        in_specs=(
            P(("group", "dec"), "tp"),
            P("tp"),
            P("tp", None),
            P(),
            P(),
            P(),
            P(("group", "dec"), "tp", None),
            P(("group", "dec"), None, "tp", None),
            P(("group", "dec"), None, "tp", None),
            P(("group", "dec"), None, None),
            P("tp", None, None),
            P("tp", None, None),
        ),
        out_specs=(P(("group", "dec"), None), P(("group", "dec"), None, "tp", None)),
        check_vma=False,
    )
```

```python
import math

import jax
import jax.numpy as jnp
from jax import lax
from jax.experimental import pallas as pl
from jax.experimental.pallas import tpu as pltpu
from jax.sharding import PartitionSpec as P

D = 7168
EPSILON = 1e-06
LAT = 512
ROW = 576
SEG = 512
SPAN = 384
REQS = 12
QPR = 16
HALF = 6
NQ = HALF * QPR
MSG = NQ + 16
SPLIT = 48
PIECE = 96
LAST = (HALF - 1) * QPR
LOG2 = math.log2(math.e) / math.sqrt(192.0)
HIDE = -(2.0**99)
FLOOR = -(2.0**60)
F32 = jnp.float32
BF16 = jnp.bfloat16


def dot_nt(a, b):
    return lax.dot_general(a, b, (((1,), (1,)), ((), ())), preferred_element_type=F32)


def shift(value, dz, dx):
    pairs = [
        (z * 4 + x, (z + dz) % 8 * 4 + (x + dx) % 4) for z in range(8) for x in range(4)
    ]
    return lax.ppermute(value, "tp", pairs)


def gather_z(value):
    groups = [[z * 4 + x for z in range(8)] for x in range(4)]
    return lax.all_gather(value, "tp", axis=0, axis_index_groups=groups)


def params(mib):
    return pltpu.CompilerParams(vmem_limit_bytes=mib * 1024 * 1024)


def vmem():
    return pl.BlockSpec(memory_space=pltpu.VMEM)


def in_hbm(value):
    return pltpu.with_memory_space_constraint(value, pltpu.HBM)


def copy_all(sources, targets, sems):
    copies = [
        pltpu.make_async_copy(source, target, sems.at[k])
        for k, (source, target) in enumerate(zip(sources, targets))
    ]
    for copy in copies:
        copy.start()
    for copy in copies:
        copy.wait()


def smem():
    return pl.BlockSpec(memory_space=pltpu.SMEM)


def two_terms(value):
    high = value.astype(BF16).astype(F32)
    return high, (value - high).astype(BF16).astype(F32)


def place_rows(rows, first=0):
    index = lax.broadcasted_iota(jnp.int32, (16, 128), 0)
    block = jnp.zeros((16, 128), F32)
    for k, row in enumerate(rows):
        block = jnp.where(index == first + k, row, block)
    return block


def eye_rows():
    a = lax.broadcasted_iota(jnp.int32, (128, 128), 0)
    b = lax.broadcasted_iota(jnp.int32, (128, 128), 1)
    return (a == b).astype(F32).astype(BF16)


def pick_rows(first):
    a = lax.broadcasted_iota(jnp.int32, (16, 128), 0)
    b = lax.broadcasted_iota(jnp.int32, (16, 128), 1)
    return ((a == b + first) & (b < 4)).astype(F32).astype(BF16)


def soften(scores):
    top = jnp.maximum(jnp.max(scores, -1, keepdims=True) * LOG2, FLOOR)
    high, low = two_terms(top)
    weights = jnp.exp2(scores * LOG2 - (high + low))
    total_high, total_low = two_terms(jnp.sum(weights, -1, keepdims=True))
    lane = lax.broadcasted_iota(jnp.int32, (scores.shape[0], 128), 1)
    stats = jnp.where(
        lane == 0,
        high,
        jnp.where(
            lane == 1,
            low,
            jnp.where(lane == 2, total_high, jnp.where(lane == 3, total_low, 0.0)),
        ),
    ).astype(BF16)
    return weights.astype(BF16), stats


def work_order(place_ref):
    place = jnp.int32(0)
    for g in range(8):
        request = place_ref[2 + g]
        place = jnp.where(
            lax.div(request, REQS) == place_ref[1], lax.rem(request, REQS), place
        )
    return [lax.rem(place + REQS - HALF + 1 + i, REQS) for i in range(REQS)]


def prepare(place, hidden_t, in_gain, kv_weight, q_nope, q_rope, key_absorb):
    def kernel(
        place_ref, gain_ref, hidden_hbm, weight_hbm, nope_hbm, rope_hbm, key_hbm,
        x_ref, z_ref, own_ref, *rest,
    ):
        sends, scratch, sems = rest[:3], rest[3], rest[9]
        hidden_ref, weight_ref, nope_ref, rope_ref, key_ref = rest[4:9]
        copies = [
            pltpu.make_async_copy(source, target, sems.at[k])
            for k, (source, target) in enumerate(
                (
                    (nope_hbm, nope_ref),
                    (key_hbm, key_ref),
                    (rope_hbm, rope_ref),
                    (hidden_hbm, hidden_ref),
                    (weight_hbm, weight_ref),
                )
            )
        ]
        for copy in copies:
            copy.start()
        order = work_order(place_ref)
        for copy in copies[:3]:
            copy.wait()
        nope = jnp.concatenate([nope_ref[i] for i in order], 0)
        head = lax.broadcasted_iota(jnp.int32, (REQS * QPR, LAT), 0) % 4
        latent = jnp.zeros((REQS * QPR, LAT), F32)
        for h in range(4):
            part = jnp.dot(nope, key_ref[h], preferred_element_type=F32)
            latent = jnp.where(head == h, part, latent)
        latent = latent.astype(BF16)
        for out, base in ((x_ref, 0), (z_ref, HALF)):
            out[:NQ, :] = latent[base * QPR : base * QPR + NQ]
            for i in range(HALF):
                out[NQ:, 64 * i : 64 * i + 64] = rope_ref[order[base + i]]
            out[NQ:, 64 * HALF :] = jnp.zeros((16, LAT - 64 * HALF), BF16)

        for copy in copies[3:]:
            copy.wait()
        a = lax.broadcasted_iota(jnp.int32, (224, 224), 0)
        b = lax.broadcasted_iota(jnp.int32, (224, 224), 1)
        eye = (a == b).astype(F32).astype(BF16)
        gain = dot_nt(eye, jnp.broadcast_to(gain_ref[...], (16, 224)))[:, :1]
        rows = hidden_ref[...].astype(F32)
        over_rows = (((0,), (0,)), ((), ()))
        scratch[:, :ROW] = lax.dot_general(
            (rows * gain).astype(BF16), weight_ref[...], over_rows, preferred_element_type=F32
        ).astype(BF16)
        ones = jnp.ones((224, 128), BF16)
        squares = sum(
            lax.dot_general(term.astype(BF16), ones, over_rows, preferred_element_type=F32)
            for term in two_terms(rows * rows)
        )[:, :64]
        lane = lax.broadcasted_iota(jnp.int32, (SPAN, 64), 1)
        high, low = two_terms(squares)
        scratch[:, ROW:] = jnp.where(lane == 0, high, jnp.where(lane == 1, low, 0.0)).astype(BF16)
        for step, out in enumerate((own_ref, *sends)):
            start = pl.multiple_of(lax.rem(place_ref[0] + step, 4) * PIECE, PIECE)
            piece = scratch[pl.ds(start, PIECE), :]
            out[:PIECE, :] = piece[:, :LAT]
            for j in range(3):
                out[PIECE:, 128 * j : 128 * j + 128] = piece[32 * j : 32 * j + 32, LAT:]
            out[PIECE:, 384:] = jnp.zeros((32, 128), BF16)

    shard = jax.ShapeDtypeStruct((MSG, LAT), BF16)
    return pl.pallas_call(
        kernel,
        out_shape=[shard, shard] + [jax.ShapeDtypeStruct((PIECE + 32, LAT), BF16)] * 4,
        in_specs=[smem(), vmem()] + [pl.BlockSpec(memory_space=pltpu.HBM)] * 5,
        out_specs=[vmem()] * 6,
        scratch_shapes=[pltpu.VMEM((SPAN, 640), BF16)]
        + [pltpu.VMEM(v.shape, BF16) for v in (hidden_t, kv_weight, q_nope, q_rope, key_absorb)]
        + [pltpu.SemaphoreType.DMA((5,))],
        compiler_params=params(12),
        name="prepare",
    )(
        place,
        in_gain.reshape(1, -1),
        *(in_hbm(v) for v in (hidden_t, kv_weight, q_nope, q_rope, key_absorb)),
    )


def finish(total, kv_gain, cosine, sine):
    def kernel(total_ref, gain_ref, cos_ref, sin_ref, rows_ref):
        total = sum(total_ref[z].astype(F32) for z in range(8))
        tail = jnp.concatenate(
            [total[PIECE:, 128 * j : 128 * j + 128] for j in range(3)], 0
        )
        scale = lax.rsqrt((tail[:, 64:65] + tail[:, 65:66]) / D + EPSILON)
        latent = total[:PIECE] * scale
        latent = (
            latent
            * lax.rsqrt(jnp.mean(latent * latent, -1, keepdims=True) + EPSILON)
            * gain_ref[...].astype(F32)
        )
        first = tail[:, :32] * scale
        second = tail[:, 32:64] * scale
        cos, sin = cos_ref[...], sin_ref[...]
        rope = jnp.concatenate([first * cos - second * sin, first * sin + second * cos], -1)
        rows_ref[:PIECE, :] = latent.astype(BF16)
        rope = rope.astype(BF16)
        for j in range(6):
            rows_ref[PIECE:, 64 * j : 64 * j + 64] = rope[16 * j : 16 * j + 16]
        rows_ref[PIECE:, 384:] = jnp.zeros((16, 128), BF16)

    return pl.pallas_call(
        kernel,
        out_shape=jax.ShapeDtypeStruct((MSG, LAT), BF16),
        in_specs=[vmem()] * 4,
        out_specs=vmem(),
        compiler_params=params(8),
        name="finish",
    )(total, kv_gain.reshape(1, -1), cosine, sine)


def attend_span(bundle, rows):
    def kernel(query_ref, rows_ref, out_ref):
        keys = rows_ref[:PIECE, :]
        key_rope = jnp.concatenate(
            [rows_ref[PIECE:, 64 * j : 64 * j + 64] for j in range(6)], 0
        )
        lanes = 64 * (HALF - 1)
        latent = jnp.concatenate([query_ref[t, LAST:NQ, :] for t in range(4)], 0)
        rope = jnp.concatenate(
            [query_ref[t, NQ:, lanes : lanes + 64] for t in range(4)], 0
        )
        weights, stats = soften(dot_nt(latent, keys) + dot_nt(rope, key_rope))
        out_ref[: 4 * QPR, :] = jnp.dot(
            weights, keys, preferred_element_type=F32
        ).astype(BF16)
        for t in range(4):
            column = jnp.concatenate(
                [
                    jnp.zeros((LAST, 128), BF16),
                    stats[t * QPR : t * QPR + QPR],
                    jnp.zeros((128 - NQ, 128), BF16),
                ],
                0,
            )
            out_ref[4 * QPR :, 128 * t : 128 * t + 128] = dot_nt(pick_rows(0), column).astype(
                BF16
            )

    return pl.pallas_call(
        kernel,
        out_shape=jax.ShapeDtypeStruct((4 * QPR + 16, LAT), BF16),
        in_specs=[vmem()] * 2,
        out_specs=vmem(),
        compiler_params=params(8),
        name="attend_span",
    )(bundle, rows)


def unpack(x_index, own, received):
    def kernel(x_ref, *refs):
        out = refs[-1]
        for step, ref in enumerate(refs[:-1]):
            base = MSG if step else 0
            start = pl.multiple_of(lax.rem(x_ref[0] + step, 4) * PIECE, PIECE)
            out[pl.ds(start, PIECE), :LAT] = ref[base : base + PIECE, :]
            out[pl.ds(start, PIECE), LAT:] = jnp.concatenate(
                [ref[base + PIECE : base + MSG, 64 * j : 64 * j + 64] for j in range(6)], 0
            )

    return pl.pallas_call(
        kernel,
        out_shape=jax.ShapeDtypeStruct((SPAN, ROW), BF16),
        in_specs=[smem()] + [vmem()] * 4,
        out_specs=vmem(),
        compiler_params=params(8),
        name="unpack",
    )(x_index, own, *received)


def fresh(place, own_x, own_s, q_rope, new_latent):
    def kernel(place_ref, x_ref, z_ref, rope_ref, new_ref, fx_ref, fz_ref):
        order = work_order(place_ref)
        rope = jnp.concatenate([rope_ref[i] for i in order], 0)
        latent = jnp.concatenate([x_ref[:NQ, :], z_ref[:NQ, :]], 0)
        row = lax.broadcasted_iota(jnp.int32, (REQS * QPR, 4 * REQS), 0)
        column = lax.broadcasted_iota(jnp.int32, (REQS * QPR, 4 * REQS), 1)
        request = lax.rem(row // QPR + order[0], REQS)
        seen = (column // 4 == request) & (column % 4 <= (row // 4) % 4)
        scores = dot_nt(latent, new_ref[:, :LAT]) + dot_nt(rope, new_ref[:, LAT:])
        weights, stats = soften(scores + jnp.where(seen, 0.0, HIDE))
        sums = jnp.dot(weights, new_ref[:, :LAT], preferred_element_type=F32).astype(BF16)
        for out, start in ((fx_ref, 0), (fz_ref, NQ)):
            out[:NQ, :] = sums[start : start + NQ]
            padded = jnp.concatenate(
                [stats[start : start + NQ], jnp.zeros((128 - NQ, 128), BF16)], 0
            )
            out[NQ:, :128] = dot_nt(pick_rows(0), padded).astype(BF16)
            out[NQ:, 128:] = jnp.zeros((16, 384), BF16)

    return pl.pallas_call(
        kernel,
        out_shape=[jax.ShapeDtypeStruct((MSG, LAT), BF16)] * 2,
        in_specs=[smem()] + [vmem()] * 4,
        out_specs=[vmem()] * 2,
        compiler_params=params(8),
        name="fresh",
    )(place, own_x, own_s, q_rope, new_latent)


def attend(order, cache_t, bias, queries, first, sent, places=None):
    if places is None:
        counts = [q.shape[0] for q in queries]
        tables = [order]
    else:
        counts = [len(group) for group in places]
        tables = [order, jnp.stack([place for group in places for place in group])]
    slots = sum(counts)
    n, m = len(counts), len(queries) if places is None else slots
    stored = [k for k in range(n) if k not in sent]
    steps = HALF // 2

    def kernel(*refs):
        table_refs, refs = refs[: len(tables)], refs[len(tables) :]
        cache_refs, bias_refs, refs = refs[:2], refs[2:4], refs[4:]
        q_refs, results, refs = refs[:m], refs[m : m + n], refs[m + n :]
        stat_ref, sems, held = refs[0], refs[1], refs[2:]
        out_refs = [held[stored.index(k)] if k in stored else results[k] for k in range(n)]
        i = pl.program_id(0)

        @pl.when(i == 0)
        def _():
            stat_ref[...] = jnp.zeros_like(stat_ref)

        lanes = pl.ds(pl.multiple_of(i * 128, 128), 128)
        rope = jnp.concatenate(
            [q[:, NQ:, lanes].reshape(-1, 128) for q in q_refs], 0
        )
        for side in range(2):
            at = pl.multiple_of(i * (2 * QPR) + side * QPR, QPR)
            keys = cache_refs[side][0]
            bias_row = bias_refs[side][0]
            latent = jnp.concatenate(
                [q[:, pl.ds(at, QPR), :].reshape(-1, LAT) for q in q_refs], 0
            )
            turned = [keys[LAT:], jnp.zeros((64, keys.shape[1]), BF16)]
            turned = jnp.concatenate(turned if side == 0 else turned[::-1], 0)
            scores = jnp.dot(latent, keys[:LAT], preferred_element_type=F32)
            scores = scores + jnp.dot(rope, turned, preferred_element_type=F32)
            weights, stats = soften(scores + bias_row)
            sums = dot_nt(weights, keys[:LAT]).astype(BF16)
            stat_ref[:, pl.ds(at, QPR), :] = stats.reshape(slots, QPR, 128)
            k = 0
            for out, c in zip(out_refs, counts):
                for t in range(c):
                    out[pl.ds(pl.multiple_of(t * NQ + at, QPR), QPR), :] = sums[
                        k * QPR : (k + 1) * QPR
                    ]
                    k += 1

        @pl.when(i == steps - 1)
        def _():
            k = 0
            for out, c in zip(out_refs, counts):
                for group in range(4):
                    block = jnp.zeros((16, 128), F32)
                    for t in range(group, c, 4):
                        block += dot_nt(pick_rows(t // 4 * 4), stat_ref[k + t])
                    out[pl.ds(c * NQ, 16), group * 128 : group * 128 + 128] = block.astype(BF16)
                k += c
            copy_all([out_refs[k] for k in stored], [results[k] for k in stored], sems)

    def at_place(k):
        return pl.BlockSpec((1, MSG, LAT), lambda i, o, table: (table[k], 0, 0))

    def at_side(shape, side):
        return pl.BlockSpec(shape, lambda i, o, *_: (o[first + 2 * i + side], 0, 0))

    total = slots * QPR * HALF
    return pl.pallas_call(
        kernel,
        grid_spec=pltpu.PrefetchScalarGridSpec(
            num_scalar_prefetch=len(tables),
            grid=(steps,),
            in_specs=[at_side((1, ROW, SEG), side) for side in range(2)]
            + [at_side((1, 1, SEG), side) for side in range(2)]
            + [vmem() if places is None else at_place(k) for k in range(m)],
            out_specs=[
                pl.BlockSpec(memory_space=pltpu.HBM) if k in stored else vmem() for k in range(n)
            ],
            scratch_shapes=[
                pltpu.VMEM((slots, 128, 128), BF16),
                pltpu.SemaphoreType.DMA((max(len(stored), 1),)),
                *(pltpu.VMEM((counts[k] * NQ + 16, LAT), BF16) for k in stored),
            ],
        ),
        out_shape=[
            (pltpu.HBM if k in stored else jax.ShapeDtypeStruct)((c * NQ + 16, LAT), BF16)
            for k, c in enumerate(counts)
        ],
        compiler_params=params(20),
        cost_estimate=pl.CostEstimate(
            flops=2 * total * SEG * (ROW + LAT),
            bytes_accessed=HALF * SEG * ROW * 2 + total * (ROW + LAT) * 2,
            transcendentals=total * SEG,
        ),
        name="attend",
    )(*tables, cache_t, cache_t, bias, bias, *(queries if places is None else queries * slots))


def combine_slot(in_refs, shapes, sources, first, last):
    lane = lax.broadcasted_iota(jnp.int32, (1, 128), 1)
    tops, totals = [], []
    for which, slot in sources:
        count, low, high = shapes[which]
        base = count * (high - low)
        block = in_refs[which][base : base + 16, slot % 4 * 128 : slot % 4 * 128 + 128]
        block = block.astype(F32)
        g = slot // 4 * 4
        top = block[g : g + 1] + block[g + 1 : g + 2]
        total = block[g + 2 : g + 3] + block[g + 3 : g + 4]
        if low > first or high < last:
            inside = (lane >= low) & (lane < high)
            top = jnp.where(inside, top, FLOOR)
            total = jnp.where(inside, total, 0.0)
        tops.append(top)
        totals.append(total)
    top = tops[0]
    for other in tops[1:]:
        top = jnp.maximum(top, other)
    factors = [jnp.exp2(t - top) for t in tops]
    total = sum(f * t for f, t in zip(factors, totals))
    terms = [term for f in factors + [total] for term in two_terms(f)]
    columns = dot_nt(eye_rows(), place_rows(terms).astype(BF16))
    columns = [
        columns[:, 2 * k : 2 * k + 1] + columns[:, 2 * k + 1 : 2 * k + 2]
        for k in range(len(factors) + 1)
    ]
    cuts = {first, last}
    for which, _ in sources:
        cuts |= {max(first, shapes[which][1]), min(last, shapes[which][2])}
    cuts = sorted(cuts)
    segments = []
    for a, b in zip(cuts[:-1], cuts[1:]):
        value = None
        for (which, slot), column in zip(sources, columns):
            count, low, high = shapes[which]
            if low <= a and b <= high:
                at = slot * (high - low) + a - low
                part = in_refs[which][at : at + b - a, :].astype(F32) * column[a:b]
                value = part if value is None else value + part
        segments.append((a, b, value))
    return segments, top, total, columns[-1]


def merge(local, received, shapes, outs, append=None):
    extra = [] if append is None else [append]
    inputs = [*local, *received]
    n = len(local)

    def kernel(*refs):
        held = refs[len(refs) - n :]
        if local:
            copy_all(refs[:n], held, refs[-1 - n])
        in_refs = [*held, *refs[n : len(inputs)]]
        out_refs = refs[len(inputs) + len(extra) :][: len(outs)]
        for out, (slots, first, last, *appended) in zip(out_refs, outs):
            rows = last - first
            base = len(slots) * rows
            blocks = [jnp.zeros((16, 128), F32) for _ in range(4)]
            for t, sources in enumerate(slots):
                segments, top, total, _ = combine_slot(in_refs, shapes, sources, first, last)
                for a, b, value in segments:
                    out[t * rows + a - first : t * rows + b - first, :] = value.astype(BF16)
                stats = [*two_terms(top), *two_terms(total)]
                blocks[t % 4] += place_rows(stats, t // 4 * 4)
            for group in range(4):
                out[base : base + 16, group * 128 : group * 128 + 128] = blocks[group].astype(
                    BF16
                )
            if appended:
                out[base + 16 :, :] = refs[len(inputs)][...]

    size = sum(v.size for v in inputs)
    return pl.pallas_call(
        kernel,
        out_shape=[
            jax.ShapeDtypeStruct(
                (len(s) * (b - a) + 16 + (append.shape[0] if more else 0), LAT), BF16
            )
            for s, a, b, *more in outs
        ],
        in_specs=[pl.BlockSpec(memory_space=pltpu.HBM)] * n
        + [vmem()] * (len(received) + len(extra)),
        out_specs=[vmem()] * len(outs),
        scratch_shapes=[
            pltpu.SemaphoreType.DMA((max(n, 1),)),
            *(pltpu.VMEM(v.shape, BF16) for v in local),
        ],
        compiler_params=params(8),
        cost_estimate=pl.CostEstimate(
            flops=4 * size, bytes_accessed=4 * size, transcendentals=0
        ),
        name="merge",
    )(*(in_hbm(v) for v in local), *received, *extra)


def conclude(order, x_messages, s_messages, value_absorb):
    nx = len(x_messages)

    def kernel(order_ref, value_ref, *refs):
        out = refs[-1]
        parts = []
        for messages in (refs[:nx], refs[nx:-1]):
            shapes = [(1, 0, NQ)] * len(messages)
            sources = [(k, 0) for k in range(len(messages))]
            segments, _, _, column = combine_slot(messages, shapes, sources, 0, NQ)
            parts.append((segments[0][2] / column[:NQ]).astype(BF16))
        mixed = jnp.concatenate(parts, 0)
        head = lax.broadcasted_iota(jnp.int32, (REQS * QPR, 128), 0) % 4
        result = jnp.zeros((REQS * QPR, 128), F32)
        for h in range(4):
            part = jnp.dot(mixed, value_ref[h], preferred_element_type=F32)
            result = jnp.where(head == h, part, result)
        result = result.astype(BF16)
        for i in range(REQS):
            out[order_ref[i]] = result[i * QPR : (i + 1) * QPR]

    return pl.pallas_call(
        kernel,
        out_shape=jax.ShapeDtypeStruct((REQS, QPR, 128), BF16),
        in_specs=[smem()] + [vmem()] * (1 + len(x_messages) + len(s_messages)),
        out_specs=vmem(),
        compiler_params=params(8),
        name="conclude",
    )(order, value_absorb, *x_messages, *s_messages)


def per_device(
    hidden,
    in_gain,
    kv_weight,
    kv_gain,
    span_req,
    lengths,
    cache,
    q_nope,
    q_rope,
    new_latent,
    key_absorb,
    value_absorb,
):
    tp_index = lax.axis_index("tp")
    z_index, x_index = tp_index // 4, tp_index % 4
    group_index, dec_index = lax.axis_index("group"), lax.axis_index("dec")
    shard_index = group_index * 2 + dec_index
    places = jnp.concatenate([jnp.stack([x_index, shard_index]).astype(jnp.int32), span_req])
    rope = q_rope.reshape(REQS, QPR, 64)
    own_x, own_s, piece, send1, send2, send3 = prepare(
        places,
        hidden.T,
        in_gain,
        kv_weight,
        q_nope.reshape(REQS, QPR, 128),
        rope,
        key_absorb,
    )

    gathered = lax.all_gather(own_s, "tp", axis=0)

    bundle = jnp.stack(
        [own_x, shift(own_x, 0, 1), shift(own_x, 0, -1), shift(own_x, 0, 2)]
    )
    bundle, send1, send2, send3 = lax.optimization_barrier((bundle, send1, send2, send3))
    total = piece.astype(F32)
    for received in (shift(send1, 0, 1), shift(send3, 0, -1), shift(send2, 0, 2)):
        total = total + received.astype(F32)
    total = gather_z(total.astype(BF16))
    up = [bundle]
    down = [bundle]
    for _ in range(3):
        up.append(shift(up[-1], 1, 0))
        down.append(shift(down[-1], -1, 0))
    table = jnp.arange(lengths.shape[0], dtype=jnp.int32)
    spans = jnp.arange(span_req.shape[0], dtype=jnp.int32)
    span_lengths = jnp.sum(
        jnp.where(span_req[:, None] == table[None, :], lengths[None, :], 0), -1
    )
    here = span_req // REQS == shard_index
    source = jnp.sum(jnp.where(here, spans, 0))
    place = jnp.sum(jnp.where(here, span_req % REQS, 0))
    span_start = jnp.sum(jnp.where(here, span_lengths, 0)) - SPAN
    order = (place + REQS - HALF + 1 + jnp.arange(REQS, dtype=jnp.int32)) % REQS
    positions = tp_index * SEG + jnp.arange(SEG, dtype=jnp.int32)
    my_lengths = lax.dynamic_slice_in_dim(lengths, shard_index * REQS, REQS)
    replaced = (positions >= span_start) & (positions < span_start + SPAN)
    is_span = jnp.arange(REQS) == place
    visible = (positions[None, :] < my_lengths[:, None]) & ~(
        is_span[:, None] & replaced[None, :]
    )
    bias = jnp.where(visible, 0.0, HIDE).astype(F32)[:, None, :]

    fresh_x, fresh_s = fresh(places, own_x, own_s, rope, new_latent.reshape(REQS * 4, ROW))

    cache_t = pltpu.with_memory_space_constraint(jnp.swapaxes(cache, 1, 2), pltpu.HBM)
    low = attend(order, cache_t, bias, [bundle, up[1], down[1], up[2], down[2]], 0, ())
    up[3], down[3], low, fresh_x, fresh_s = lax.optimization_barrier(
        (up[3], down[3], low, fresh_x, fresh_s)
    )
    up.append(shift(up[3][:2], 1, 0))
    down.append(shift(down[3][2:], -1, 0))
    top = attend(order, cache_t, bias, [up[3], down[3], up[4], down[4]], 0, (2, 3))

    def column(dx):
        steps = (0, -1, 1, -2, 2, -3, 3, 4)
        return [(z_index + dz) % 8 * 4 + (x_index + dx) % 4 for dz in steps]

    across = column(2)
    gathered = in_hbm(gathered)
    ends = attend(order, cache_t, bias, [gathered], HALF, (0, 1), [across[:4], across[4:]])
    wide = attend(
        order, cache_t, bias, [gathered], HALF, (), [column(0), column(-1), column(1)]
    )

    eight = (8, 0, NQ)
    from_right = shift(ends[0], 0, -1)
    from_left = shift(ends[1], 0, 1)
    right_sum, left_sum = merge(
        [wide[1], wide[2]],
        [from_right, from_left],
        [eight, eight, (4, 0, NQ), (4, 0, NQ)],
        [
            ([[(0, t), (2, t)] for t in range(4)] + [[(0, t)] for t in range(4, 8)], 0, NQ),
            ([[(1, t)] for t in range(4)] + [[(1, t), (3, t - 4)] for t in range(4, 8)], 0, NQ),
        ],
    )
    four = (4, 0, NQ)
    two = (2, 0, NQ)
    from_up = shift(top[2], -1, 0)
    from_down = shift(top[3], 1, 0)
    up_sum, down_sum = merge(
        [top[0], top[1]],
        [from_up, from_down],
        [four, four, two, two],
        [
            ([[(0, 0), (2, 0)], [(0, 1), (2, 1)], [(0, 2)], [(0, 3)]], 0, NQ),
            ([[(1, 0)], [(1, 1)], [(1, 2), (3, 0)], [(1, 3), (3, 1)]], 0, NQ),
        ],
    )
    for level in (2, 1):
        from_up = shift(up_sum, -1, 0)
        from_down = shift(down_sum, 1, 0)
        if level == 2:
            from_up, from_down, right_sum, left_sum = lax.optimization_barrier(
                (from_up, from_down, right_sum, left_sum)
            )
        up_sum, down_sum = merge(
            [low[2 * level - 1], low[2 * level]],
            [from_up, from_down],
            [four] * 4,
            [
                ([[(0, t), (2, t)] for t in range(4)], 0, NQ),
                ([[(1, t), (3, t)] for t in range(4)], 0, NQ),
            ],
        )
    up_sum, down_sum, total = lax.optimization_barrier((up_sum, down_sum, total))
    from_up = shift(up_sum, -1, 0)
    from_down = shift(down_sum, 1, 0)

    span_me = jnp.sum(jnp.where(spans == shard_index, span_lengths, 0)) - SPAN
    row_positions = span_me + x_index * PIECE + jnp.arange(PIECE, dtype=jnp.int32)
    frequency = jnp.exp(jnp.arange(32, dtype=F32) * (-math.log(10000.0) / 32))
    angles = row_positions.astype(F32)[:, None] * frequency[None, :]
    rows = finish(total, kv_gain, jnp.cos(angles), jnp.sin(angles))
    near = jnp.stack([rows, lax.ppermute(rows, "dec", [(0, 1), (1, 0)])])
    around = [near] + [
        lax.ppermute(near, "group", [(g, (g + step) % 4) for g in range(4)])
        for step in range(1, 4)
    ]
    which = (group_index - source // 2) % 4 * 2 + (dec_index ^ (source % 2))
    span_rows = lax.dynamic_index_in_dim(jnp.concatenate(around, 0), which, 0, keepdims=False)
    span_part = attend_span(bundle, span_rows)

    own = merge(
        [low[0]],
        [from_up, from_down, span_part],
        [four] * 3 + [(4, LAST, NQ)],
        [
            ([[(0, t), (1, t), (2, t), (3, t)]], 0, NQ, *((True,) if t else ()))
            for t in range(4)
        ],
        rows,
    )
    x_received = [shift(own[2], 0, 1), shift(own[1], 0, -1), shift(own[3], 0, 2)]

    from_right = shift(right_sum, 0, -1)
    from_left = shift(left_sum, 0, 1)
    every = lambda t: [[(0, t), (1, t), (2, t)]]
    mine, rise1, fall1, rise2, fall2, rise3, fall3, far_up, far_down = merge(
        [wide[0]],
        [from_right, from_left],
        [eight] * 3,
        [(every(t), 0, NQ) for t in range(7)] + [(every(7), 0, SPLIT), (every(7), SPLIT, NQ)],
    )
    unit = (1, 0, NQ)
    pair = [([[(0, 0), (2, 0)]], 0, NQ), ([[(1, 0), (3, 0)]], 0, NQ)]
    rise_sum, fall_sum = merge(
        [],
        [rise3, fall3, shift(far_up, -1, 0), shift(far_down, 1, 0)],
        [unit, unit, (1, 0, SPLIT), (1, SPLIT, NQ)],
        pair,
    )
    for rise_own, fall_own in ((rise2, fall2), (rise1, fall1)):
        rise_sum, fall_sum = merge(
            [],
            [rise_own, fall_own, shift(rise_sum, -1, 0), shift(fall_sum, 1, 0)],
            [unit] * 4,
            pair,
        )
    s_messages = [mine, shift(rise_sum, -1, 0), shift(fall_sum, 1, 0), fresh_s]

    new_rows = unpack(
        x_index.reshape(1), rows, [x_received[1], x_received[2], x_received[0]]
    )
    attended = conclude(order, [own[0], *x_received, fresh_x], s_messages, value_absorb)
    return (new_rows, attended.reshape(REQS, 4, 4, 128))


def solution(mesh):
    return jax.shard_map(
        per_device,
        mesh=mesh,
        in_specs=(
            P(("group", "dec"), "tp"),
            P("tp"),
            P("tp", None),
            P(),
            P(),
            P(),
            P(("group", "dec"), "tp", None),
            P(("group", "dec"), None, "tp", None),
            P(("group", "dec"), None, "tp", None),
            P(("group", "dec"), None, None),
            P("tp", None, None),
            P("tp", None, None),
        ),
        out_specs=(P(("group", "dec"), None), P(("group", "dec"), None, "tp", None)),
        check_vma=False,
    )
```

```python
import math

import jax
import jax.numpy as jnp
from jax import lax
from jax.experimental import pallas as pl
from jax.experimental.pallas import tpu as pltpu
from jax.sharding import PartitionSpec as P

D = 7168
EPSILON = 1e-06
LAT = 512
ROW = 576
SEG = 512
SPAN = 384
REQS = 12
QPR = 16
HALF = 6
NQ = HALF * QPR
MSG = NQ + 16
SPLIT = 48
PIECE = 96
LAST = (HALF - 1) * QPR
LOG2 = math.log2(math.e) / math.sqrt(192.0)
HIDE = -(2.0**99)
FLOOR = -(2.0**60)
F32 = jnp.float32
BF16 = jnp.bfloat16


def dot_nt(a, b):
    return lax.dot_general(a, b, (((1,), (1,)), ((), ())), preferred_element_type=F32)


def shift(value, dz, dx):
    pairs = [
        (z * 4 + x, (z + dz) % 8 * 4 + (x + dx) % 4) for z in range(8) for x in range(4)
    ]
    return lax.ppermute(value, "tp", pairs)


def gather_z(value):
    groups = [[z * 4 + x for z in range(8)] for x in range(4)]
    return lax.all_gather(value, "tp", axis=0, axis_index_groups=groups)


def params(mib):
    return pltpu.CompilerParams(vmem_limit_bytes=mib * 1024 * 1024)


def vmem():
    return pl.BlockSpec(memory_space=pltpu.VMEM)


def in_hbm(value):
    return pltpu.with_memory_space_constraint(value, pltpu.HBM)


def copy_all(sources, targets, sems):
    copies = [
        pltpu.make_async_copy(source, target, sems.at[k])
        for k, (source, target) in enumerate(zip(sources, targets))
    ]
    for copy in copies:
        copy.start()
    for copy in copies:
        copy.wait()


def smem():
    return pl.BlockSpec(memory_space=pltpu.SMEM)


def two_terms(value):
    high = value.astype(BF16).astype(F32)
    return high, (value - high).astype(BF16).astype(F32)


def place_rows(rows, first=0):
    index = lax.broadcasted_iota(jnp.int32, (16, 128), 0)
    block = jnp.zeros((16, 128), F32)
    for k, row in enumerate(rows):
        block = jnp.where(index == first + k, row, block)
    return block


def eye_rows():
    a = lax.broadcasted_iota(jnp.int32, (128, 128), 0)
    b = lax.broadcasted_iota(jnp.int32, (128, 128), 1)
    return (a == b).astype(F32).astype(BF16)


def pick_rows(first):
    a = lax.broadcasted_iota(jnp.int32, (16, 128), 0)
    b = lax.broadcasted_iota(jnp.int32, (16, 128), 1)
    return ((a == b + first) & (b < 4)).astype(F32).astype(BF16)


def soften(scores):
    top = jnp.maximum(jnp.max(scores, -1, keepdims=True) * LOG2, FLOOR)
    high, low = two_terms(top)
    weights = jnp.exp2(scores * LOG2 - (high + low))
    total_high, total_low = two_terms(jnp.sum(weights, -1, keepdims=True))
    lane = lax.broadcasted_iota(jnp.int32, (scores.shape[0], 128), 1)
    stats = jnp.where(
        lane == 0,
        high,
        jnp.where(
            lane == 1,
            low,
            jnp.where(lane == 2, total_high, jnp.where(lane == 3, total_low, 0.0)),
        ),
    ).astype(BF16)
    return weights.astype(BF16), stats


def work_order(place_ref):
    place = jnp.int32(0)
    for g in range(8):
        request = place_ref[2 + g]
        place = jnp.where(
            lax.div(request, REQS) == place_ref[1], lax.rem(request, REQS), place
        )
    return [lax.rem(place + REQS - HALF + 1 + i, REQS) for i in range(REQS)]


def prepare(place, hidden_t, in_gain, kv_weight, q_nope, q_rope, key_absorb):
    def kernel(
        place_ref, gain_ref, hidden_hbm, weight_hbm, nope_hbm, rope_hbm, key_hbm,
        x_ref, z_ref, own_ref, *rest,
    ):
        sends, scratch, sems = rest[:3], rest[3], rest[9]
        hidden_ref, weight_ref, nope_ref, rope_ref, key_ref = rest[4:9]
        copies = [
            pltpu.make_async_copy(source, target, sems.at[k])
            for k, (source, target) in enumerate(
                (
                    (nope_hbm, nope_ref),
                    (key_hbm, key_ref),
                    (rope_hbm, rope_ref),
                    (hidden_hbm, hidden_ref),
                    (weight_hbm, weight_ref),
                )
            )
        ]
        for copy in copies:
            copy.start()
        order = work_order(place_ref)
        for copy in copies[:3]:
            copy.wait()
        nope = jnp.concatenate([nope_ref[i] for i in order], 0)
        head = lax.broadcasted_iota(jnp.int32, (REQS * QPR, LAT), 0) % 4
        latent = jnp.zeros((REQS * QPR, LAT), F32)
        for h in range(4):
            part = jnp.dot(nope, key_ref[h], preferred_element_type=F32)
            latent = jnp.where(head == h, part, latent)
        latent = latent.astype(BF16)
        for out, base in ((x_ref, 0), (z_ref, HALF)):
            out[:NQ, :] = latent[base * QPR : base * QPR + NQ]
            for i in range(HALF):
                out[NQ:, 64 * i : 64 * i + 64] = rope_ref[order[base + i]]
            out[NQ:, 64 * HALF :] = jnp.zeros((16, LAT - 64 * HALF), BF16)

        for copy in copies[3:]:
            copy.wait()
        a = lax.broadcasted_iota(jnp.int32, (224, 224), 0)
        b = lax.broadcasted_iota(jnp.int32, (224, 224), 1)
        eye = (a == b).astype(F32).astype(BF16)
        gain = dot_nt(eye, jnp.broadcast_to(gain_ref[...], (16, 224)))[:, :1]
        rows = hidden_ref[...].astype(F32)
        over_rows = (((0,), (0,)), ((), ()))
        scratch[:, :ROW] = lax.dot_general(
            (rows * gain).astype(BF16), weight_ref[...], over_rows, preferred_element_type=F32
        ).astype(BF16)
        ones = jnp.ones((224, 128), BF16)
        squares = sum(
            lax.dot_general(term.astype(BF16), ones, over_rows, preferred_element_type=F32)
            for term in two_terms(rows * rows)
        )[:, :64]
        lane = lax.broadcasted_iota(jnp.int32, (SPAN, 64), 1)
        high, low = two_terms(squares)
        scratch[:, ROW:] = jnp.where(lane == 0, high, jnp.where(lane == 1, low, 0.0)).astype(BF16)
        for step, out in enumerate((own_ref, *sends)):
            start = pl.multiple_of(lax.rem(place_ref[0] + step, 4) * PIECE, PIECE)
            piece = scratch[pl.ds(start, PIECE), :]
            out[:PIECE, :] = piece[:, :LAT]
            for j in range(3):
                out[PIECE:, 128 * j : 128 * j + 128] = piece[32 * j : 32 * j + 32, LAT:]
            out[PIECE:, 384:] = jnp.zeros((32, 128), BF16)

    shard = jax.ShapeDtypeStruct((MSG, LAT), BF16)
    return pl.pallas_call(
        kernel,
        out_shape=[shard, shard] + [jax.ShapeDtypeStruct((PIECE + 32, LAT), BF16)] * 4,
        in_specs=[smem(), vmem()] + [pl.BlockSpec(memory_space=pltpu.HBM)] * 5,
        out_specs=[vmem()] * 6,
        scratch_shapes=[pltpu.VMEM((SPAN, 640), BF16)]
        + [pltpu.VMEM(v.shape, BF16) for v in (hidden_t, kv_weight, q_nope, q_rope, key_absorb)]
        + [pltpu.SemaphoreType.DMA((5,))],
        compiler_params=params(12),
        name="prepare",
    )(
        place,
        in_gain.reshape(1, -1),
        *(in_hbm(v) for v in (hidden_t, kv_weight, q_nope, q_rope, key_absorb)),
    )


def finish(total, kv_gain, cosine, sine):
    def kernel(total_ref, gain_ref, cos_ref, sin_ref, rows_ref):
        total = sum(total_ref[z].astype(F32) for z in range(8))
        tail = jnp.concatenate(
            [total[PIECE:, 128 * j : 128 * j + 128] for j in range(3)], 0
        )
        scale = lax.rsqrt((tail[:, 64:65] + tail[:, 65:66]) / D + EPSILON)
        latent = total[:PIECE] * scale
        latent = (
            latent
            * lax.rsqrt(jnp.mean(latent * latent, -1, keepdims=True) + EPSILON)
            * gain_ref[...].astype(F32)
        )
        first = tail[:, :32] * scale
        second = tail[:, 32:64] * scale
        cos, sin = cos_ref[...], sin_ref[...]
        rope = jnp.concatenate([first * cos - second * sin, first * sin + second * cos], -1)
        rows_ref[:PIECE, :] = latent.astype(BF16)
        rope = rope.astype(BF16)
        for j in range(6):
            rows_ref[PIECE:, 64 * j : 64 * j + 64] = rope[16 * j : 16 * j + 16]
        rows_ref[PIECE:, 384:] = jnp.zeros((16, 128), BF16)

    return pl.pallas_call(
        kernel,
        out_shape=jax.ShapeDtypeStruct((MSG, LAT), BF16),
        in_specs=[vmem()] * 4,
        out_specs=vmem(),
        compiler_params=params(8),
        name="finish",
    )(total, kv_gain.reshape(1, -1), cosine, sine)


def attend_span(bundle, rows):
    def kernel(query_ref, rows_ref, out_ref):
        keys = rows_ref[:PIECE, :]
        key_rope = jnp.concatenate(
            [rows_ref[PIECE:, 64 * j : 64 * j + 64] for j in range(6)], 0
        )
        lanes = 64 * (HALF - 1)
        latent = jnp.concatenate([query_ref[t, LAST:NQ, :] for t in range(4)], 0)
        rope = jnp.concatenate(
            [query_ref[t, NQ:, lanes : lanes + 64] for t in range(4)], 0
        )
        weights, stats = soften(dot_nt(latent, keys) + dot_nt(rope, key_rope))
        out_ref[: 4 * QPR, :] = jnp.dot(
            weights, keys, preferred_element_type=F32
        ).astype(BF16)
        for t in range(4):
            column = jnp.concatenate(
                [
                    jnp.zeros((LAST, 128), BF16),
                    stats[t * QPR : t * QPR + QPR],
                    jnp.zeros((128 - NQ, 128), BF16),
                ],
                0,
            )
            out_ref[4 * QPR :, 128 * t : 128 * t + 128] = dot_nt(pick_rows(0), column).astype(
                BF16
            )

    return pl.pallas_call(
        kernel,
        out_shape=jax.ShapeDtypeStruct((4 * QPR + 16, LAT), BF16),
        in_specs=[vmem()] * 2,
        out_specs=vmem(),
        compiler_params=params(8),
        name="attend_span",
    )(bundle, rows)


def unpack(x_index, own, received):
    def kernel(x_ref, *refs):
        out = refs[-1]
        for step, ref in enumerate(refs[:-1]):
            base = MSG if step else 0
            start = pl.multiple_of(lax.rem(x_ref[0] + step, 4) * PIECE, PIECE)
            out[pl.ds(start, PIECE), :LAT] = ref[base : base + PIECE, :]
            out[pl.ds(start, PIECE), LAT:] = jnp.concatenate(
                [ref[base + PIECE : base + MSG, 64 * j : 64 * j + 64] for j in range(6)], 0
            )

    return pl.pallas_call(
        kernel,
        out_shape=jax.ShapeDtypeStruct((SPAN, ROW), BF16),
        in_specs=[smem()] + [vmem()] * 4,
        out_specs=vmem(),
        compiler_params=params(8),
        name="unpack",
    )(x_index, own, *received)


def fresh(place, own_x, own_s, q_rope, new_latent):
    def kernel(place_ref, x_ref, z_ref, rope_ref, new_ref, fx_ref, fz_ref):
        order = work_order(place_ref)
        rope = jnp.concatenate([rope_ref[i] for i in order], 0)
        latent = jnp.concatenate([x_ref[:NQ, :], z_ref[:NQ, :]], 0)
        row = lax.broadcasted_iota(jnp.int32, (REQS * QPR, 4 * REQS), 0)
        column = lax.broadcasted_iota(jnp.int32, (REQS * QPR, 4 * REQS), 1)
        request = lax.rem(row // QPR + order[0], REQS)
        seen = (column // 4 == request) & (column % 4 <= (row // 4) % 4)
        scores = dot_nt(latent, new_ref[:, :LAT]) + dot_nt(rope, new_ref[:, LAT:])
        weights, stats = soften(scores + jnp.where(seen, 0.0, HIDE))
        sums = jnp.dot(weights, new_ref[:, :LAT], preferred_element_type=F32).astype(BF16)
        for out, start in ((fx_ref, 0), (fz_ref, NQ)):
            out[:NQ, :] = sums[start : start + NQ]
            padded = jnp.concatenate(
                [stats[start : start + NQ], jnp.zeros((128 - NQ, 128), BF16)], 0
            )
            out[NQ:, :128] = dot_nt(pick_rows(0), padded).astype(BF16)
            out[NQ:, 128:] = jnp.zeros((16, 384), BF16)

    return pl.pallas_call(
        kernel,
        out_shape=[jax.ShapeDtypeStruct((MSG, LAT), BF16)] * 2,
        in_specs=[smem()] + [vmem()] * 4,
        out_specs=[vmem()] * 2,
        compiler_params=params(8),
        name="fresh",
    )(place, own_x, own_s, q_rope, new_latent)


def attend(order, cache_t, bias, queries, first, sent, places=None):
    if places is None:
        counts = [q.shape[0] for q in queries]
        tables = [order]
    else:
        counts = [len(group) for group in places]
        tables = [order, jnp.stack([place for group in places for place in group])]
    slots = sum(counts)
    n, m = len(counts), len(queries) if places is None else slots
    stored = [k for k in range(n) if k not in sent]
    steps = HALF // 2

    def kernel(*refs):
        table_refs, refs = refs[: len(tables)], refs[len(tables) :]
        cache_refs, bias_refs, refs = refs[:2], refs[2:4], refs[4:]
        q_refs, results, refs = refs[:m], refs[m : m + n], refs[m + n :]
        stat_ref, sems, held = refs[0], refs[1], refs[2:]
        out_refs = [held[stored.index(k)] if k in stored else results[k] for k in range(n)]
        i = pl.program_id(0)

        @pl.when(i == 0)
        def _():
            stat_ref[...] = jnp.zeros_like(stat_ref)

        lanes = pl.ds(pl.multiple_of(i * 128, 128), 128)
        rope = jnp.concatenate(
            [q[:, NQ:, lanes].reshape(-1, 128) for q in q_refs], 0
        )
        for side in range(2):
            at = pl.multiple_of(i * (2 * QPR) + side * QPR, QPR)
            keys = cache_refs[side][0]
            bias_row = bias_refs[side][0]
            latent = jnp.concatenate(
                [q[:, pl.ds(at, QPR), :].reshape(-1, LAT) for q in q_refs], 0
            )
            turned = [keys[LAT:], jnp.zeros((64, keys.shape[1]), BF16)]
            turned = jnp.concatenate(turned if side == 0 else turned[::-1], 0)
            scores = jnp.dot(latent, keys[:LAT], preferred_element_type=F32)
            scores = scores + jnp.dot(rope, turned, preferred_element_type=F32)
            weights, stats = soften(scores + bias_row)
            sums = dot_nt(weights, keys[:LAT]).astype(BF16)
            stat_ref[:, pl.ds(at, QPR), :] = stats.reshape(slots, QPR, 128)
            k = 0
            for out, c in zip(out_refs, counts):
                for t in range(c):
                    out[pl.ds(pl.multiple_of(t * NQ + at, QPR), QPR), :] = sums[
                        k * QPR : (k + 1) * QPR
                    ]
                    k += 1

        @pl.when(i == steps - 1)
        def _():
            k = 0
            for out, c in zip(out_refs, counts):
                for group in range(4):
                    block = jnp.zeros((16, 128), F32)
                    for t in range(group, c, 4):
                        block += dot_nt(pick_rows(t // 4 * 4), stat_ref[k + t])
                    out[pl.ds(c * NQ, 16), group * 128 : group * 128 + 128] = block.astype(BF16)
                k += c
            copy_all([out_refs[k] for k in stored], [results[k] for k in stored], sems)

    def at_place(k):
        return pl.BlockSpec((1, MSG, LAT), lambda i, o, table: (table[k], 0, 0))

    def at_side(shape, side):
        return pl.BlockSpec(shape, lambda i, o, *_: (o[first + 2 * i + side], 0, 0))

    total = slots * QPR * HALF
    return pl.pallas_call(
        kernel,
        grid_spec=pltpu.PrefetchScalarGridSpec(
            num_scalar_prefetch=len(tables),
            grid=(steps,),
            in_specs=[at_side((1, ROW, SEG), side) for side in range(2)]
            + [at_side((1, 1, SEG), side) for side in range(2)]
            + [vmem() if places is None else at_place(k) for k in range(m)],
            out_specs=[
                pl.BlockSpec(memory_space=pltpu.HBM) if k in stored else vmem() for k in range(n)
            ],
            scratch_shapes=[
                pltpu.VMEM((slots, 128, 128), BF16),
                pltpu.SemaphoreType.DMA((max(len(stored), 1),)),
                *(pltpu.VMEM((counts[k] * NQ + 16, LAT), BF16) for k in stored),
            ],
        ),
        out_shape=[
            (pltpu.HBM if k in stored else jax.ShapeDtypeStruct)((c * NQ + 16, LAT), BF16)
            for k, c in enumerate(counts)
        ],
        compiler_params=params(20),
        cost_estimate=pl.CostEstimate(
            flops=2 * total * SEG * (ROW + LAT),
            bytes_accessed=HALF * SEG * ROW * 2 + total * (ROW + LAT) * 2,
            transcendentals=total * SEG,
        ),
        name="attend",
    )(*tables, cache_t, cache_t, bias, bias, *(queries if places is None else queries * slots))


def combine_slot(in_refs, shapes, sources, first, last):
    lane = lax.broadcasted_iota(jnp.int32, (1, 128), 1)
    tops, totals = [], []
    for which, slot in sources:
        count, low, high = shapes[which]
        base = count * (high - low)
        block = in_refs[which][base : base + 16, slot % 4 * 128 : slot % 4 * 128 + 128]
        block = block.astype(F32)
        g = slot // 4 * 4
        top = block[g : g + 1] + block[g + 1 : g + 2]
        total = block[g + 2 : g + 3] + block[g + 3 : g + 4]
        if low > first or high < last:
            inside = (lane >= low) & (lane < high)
            top = jnp.where(inside, top, FLOOR)
            total = jnp.where(inside, total, 0.0)
        tops.append(top)
        totals.append(total)
    top = tops[0]
    for other in tops[1:]:
        top = jnp.maximum(top, other)
    factors = [jnp.exp2(t - top) for t in tops]
    total = sum(f * t for f, t in zip(factors, totals))
    terms = [term for f in factors + [total] for term in two_terms(f)]
    columns = dot_nt(eye_rows(), place_rows(terms).astype(BF16))
    columns = [
        columns[:, 2 * k : 2 * k + 1] + columns[:, 2 * k + 1 : 2 * k + 2]
        for k in range(len(factors) + 1)
    ]
    cuts = {first, last}
    for which, _ in sources:
        cuts |= {max(first, shapes[which][1]), min(last, shapes[which][2])}
    cuts = sorted(cuts)
    segments = []
    for a, b in zip(cuts[:-1], cuts[1:]):
        value = None
        for (which, slot), column in zip(sources, columns):
            count, low, high = shapes[which]
            if low <= a and b <= high:
                at = slot * (high - low) + a - low
                part = in_refs[which][at : at + b - a, :].astype(F32) * column[a:b]
                value = part if value is None else value + part
        segments.append((a, b, value))
    return segments, top, total, columns[-1]


def merge(local, received, shapes, outs, append=None):
    extra = [] if append is None else [append]
    inputs = [*local, *received]
    n = len(local)

    def kernel(*refs):
        held = refs[len(refs) - n :]
        if local:
            copy_all(refs[:n], held, refs[-1 - n])
        in_refs = [*held, *refs[n : len(inputs)]]
        out_refs = refs[len(inputs) + len(extra) :][: len(outs)]
        for out, (slots, first, last, *appended) in zip(out_refs, outs):
            rows = last - first
            base = len(slots) * rows
            blocks = [jnp.zeros((16, 128), F32) for _ in range(4)]
            for t, sources in enumerate(slots):
                segments, top, total, _ = combine_slot(in_refs, shapes, sources, first, last)
                for a, b, value in segments:
                    out[t * rows + a - first : t * rows + b - first, :] = value.astype(BF16)
                stats = [*two_terms(top), *two_terms(total)]
                blocks[t % 4] += place_rows(stats, t // 4 * 4)
            for group in range(4):
                out[base : base + 16, group * 128 : group * 128 + 128] = blocks[group].astype(
                    BF16
                )
            if appended:
                out[base + 16 :, :] = refs[len(inputs)][...]

    size = sum(v.size for v in inputs)
    return pl.pallas_call(
        kernel,
        out_shape=[
            jax.ShapeDtypeStruct(
                (len(s) * (b - a) + 16 + (append.shape[0] if more else 0), LAT), BF16
            )
            for s, a, b, *more in outs
        ],
        in_specs=[pl.BlockSpec(memory_space=pltpu.HBM)] * n
        + [vmem()] * (len(received) + len(extra)),
        out_specs=[vmem()] * len(outs),
        scratch_shapes=[
            pltpu.SemaphoreType.DMA((max(n, 1),)),
            *(pltpu.VMEM(v.shape, BF16) for v in local),
        ],
        compiler_params=params(8),
        cost_estimate=pl.CostEstimate(
            flops=4 * size, bytes_accessed=4 * size, transcendentals=0
        ),
        name="merge",
    )(*(in_hbm(v) for v in local), *received, *extra)


def conclude(order, x_messages, s_messages, value_absorb):
    nx = len(x_messages)

    def kernel(order_ref, value_ref, *refs):
        out = refs[-1]
        parts = []
        for messages in (refs[:nx], refs[nx:-1]):
            shapes = [(1, 0, NQ)] * len(messages)
            sources = [(k, 0) for k in range(len(messages))]
            segments, _, _, column = combine_slot(messages, shapes, sources, 0, NQ)
            parts.append((segments[0][2] / column[:NQ]).astype(BF16))
        mixed = jnp.concatenate(parts, 0)
        head = lax.broadcasted_iota(jnp.int32, (REQS * QPR, 128), 0) % 4
        result = jnp.zeros((REQS * QPR, 128), F32)
        for h in range(4):
            part = jnp.dot(mixed, value_ref[h], preferred_element_type=F32)
            result = jnp.where(head == h, part, result)
        result = result.astype(BF16)
        for i in range(REQS):
            out[order_ref[i]] = result[i * QPR : (i + 1) * QPR]

    return pl.pallas_call(
        kernel,
        out_shape=jax.ShapeDtypeStruct((REQS, QPR, 128), BF16),
        in_specs=[smem()] + [vmem()] * (1 + len(x_messages) + len(s_messages)),
        out_specs=vmem(),
        compiler_params=params(8),
        name="conclude",
    )(order, value_absorb, *x_messages, *s_messages)


def per_device(
    hidden,
    in_gain,
    kv_weight,
    kv_gain,
    span_req,
    lengths,
    cache,
    q_nope,
    q_rope,
    new_latent,
    key_absorb,
    value_absorb,
):
    tp_index = lax.axis_index("tp")
    z_index, x_index = tp_index // 4, tp_index % 4
    group_index, dec_index = lax.axis_index("group"), lax.axis_index("dec")
    shard_index = group_index * 2 + dec_index
    places = jnp.concatenate([jnp.stack([x_index, shard_index]).astype(jnp.int32), span_req])
    rope = q_rope.reshape(REQS, QPR, 64)
    own_x, own_s, piece, send1, send2, send3 = prepare(
        places,
        hidden.T,
        in_gain,
        kv_weight,
        q_nope.reshape(REQS, QPR, 128),
        rope,
        key_absorb,
    )

    gathered = lax.all_gather(own_s, "tp", axis=0)

    bundle = jnp.stack(
        [own_x, shift(own_x, 0, 1), shift(own_x, 0, -1), shift(own_x, 0, 2)]
    )
    bundle, send1, send2, send3 = lax.optimization_barrier((bundle, send1, send2, send3))
    total = piece.astype(F32)
    for received in (shift(send1, 0, 1), shift(send3, 0, -1), shift(send2, 0, 2)):
        total = total + received.astype(F32)
    total = gather_z(total.astype(BF16))
    up = [bundle]
    down = [bundle]
    for _ in range(3):
        up.append(shift(up[-1], 1, 0))
        down.append(shift(down[-1], -1, 0))
    table = jnp.arange(lengths.shape[0], dtype=jnp.int32)
    spans = jnp.arange(span_req.shape[0], dtype=jnp.int32)
    span_lengths = jnp.sum(
        jnp.where(span_req[:, None] == table[None, :], lengths[None, :], 0), -1
    )
    here = span_req // REQS == shard_index
    source = jnp.sum(jnp.where(here, spans, 0))
    place = jnp.sum(jnp.where(here, span_req % REQS, 0))
    span_start = jnp.sum(jnp.where(here, span_lengths, 0)) - SPAN
    order = (place + REQS - HALF + 1 + jnp.arange(REQS, dtype=jnp.int32)) % REQS
    positions = tp_index * SEG + jnp.arange(SEG, dtype=jnp.int32)
    my_lengths = lax.dynamic_slice_in_dim(lengths, shard_index * REQS, REQS)
    replaced = (positions >= span_start) & (positions < span_start + SPAN)
    is_span = jnp.arange(REQS) == place
    visible = (positions[None, :] < my_lengths[:, None]) & ~(
        is_span[:, None] & replaced[None, :]
    )
    bias = jnp.where(visible, 0.0, HIDE).astype(F32)[:, None, :]

    fresh_x, fresh_s = fresh(places, own_x, own_s, rope, new_latent.reshape(REQS * 4, ROW))

    cache_t = pltpu.with_memory_space_constraint(jnp.swapaxes(cache, 1, 2), pltpu.HBM)
    low = attend(order, cache_t, bias, [bundle, up[1], down[1], up[2], down[2]], 0, ())
    up[3], down[3], low, fresh_x, fresh_s = lax.optimization_barrier(
        (up[3], down[3], low, fresh_x, fresh_s)
    )
    up.append(shift(up[3][:2], 1, 0))
    down.append(shift(down[3][2:], -1, 0))
    top = attend(order, cache_t, bias, [up[3], down[3], up[4], down[4]], 0, (2, 3))

    four = (4, 0, NQ)
    two = (2, 0, NQ)
    from_up = shift(top[2], -1, 0)
    from_down = shift(top[3], 1, 0)
    up_sum, down_sum = merge(
        [top[0], top[1]],
        [from_up, from_down],
        [four, four, two, two],
        [
            ([[(0, 0), (2, 0)], [(0, 1), (2, 1)], [(0, 2)], [(0, 3)]], 0, NQ),
            ([[(1, 0)], [(1, 1)], [(1, 2), (3, 0)], [(1, 3), (3, 1)]], 0, NQ),
        ],
    )
    gathered, up_sum, down_sum = lax.optimization_barrier((gathered, up_sum, down_sum))
    from_up = shift(up_sum, -1, 0)
    from_down = shift(down_sum, 1, 0)

    def column(dx):
        steps = (0, -1, 1, -2, 2, -3, 3, 4)
        return [(z_index + dz) % 8 * 4 + (x_index + dx) % 4 for dz in steps]

    across = column(2)
    gathered = in_hbm(gathered)
    ends = attend(order, cache_t, bias, [gathered], HALF, (0, 1), [across[:4], across[4:]])
    wide = attend(
        order, cache_t, bias, [gathered], HALF, (), [column(0), column(-1), column(1)]
    )

    eight = (8, 0, NQ)
    from_right = shift(ends[0], 0, -1)
    from_left = shift(ends[1], 0, 1)
    right_sum, left_sum = merge(
        [wide[1], wide[2]],
        [from_right, from_left],
        [eight, eight, (4, 0, NQ), (4, 0, NQ)],
        [
            ([[(0, t), (2, t)] for t in range(4)] + [[(0, t)] for t in range(4, 8)], 0, NQ),
            ([[(1, t)] for t in range(4)] + [[(1, t), (3, t - 4)] for t in range(4, 8)], 0, NQ),
        ],
    )
    from_up, from_down, right_sum, left_sum = lax.optimization_barrier(
        (from_up, from_down, right_sum, left_sum)
    )
    for level in (2, 1):
        if level == 1:
            from_up = shift(up_sum, -1, 0)
            from_down = shift(down_sum, 1, 0)
        up_sum, down_sum = merge(
            [low[2 * level - 1], low[2 * level]],
            [from_up, from_down],
            [four] * 4,
            [
                ([[(0, t), (2, t)] for t in range(4)], 0, NQ),
                ([[(1, t), (3, t)] for t in range(4)], 0, NQ),
            ],
        )
    up_sum, down_sum, total = lax.optimization_barrier((up_sum, down_sum, total))
    from_up = shift(up_sum, -1, 0)
    from_down = shift(down_sum, 1, 0)

    span_me = jnp.sum(jnp.where(spans == shard_index, span_lengths, 0)) - SPAN
    row_positions = span_me + x_index * PIECE + jnp.arange(PIECE, dtype=jnp.int32)
    frequency = jnp.exp(jnp.arange(32, dtype=F32) * (-math.log(10000.0) / 32))
    angles = row_positions.astype(F32)[:, None] * frequency[None, :]
    rows = finish(total, kv_gain, jnp.cos(angles), jnp.sin(angles))
    near = jnp.stack([rows, lax.ppermute(rows, "dec", [(0, 1), (1, 0)])])
    around = [near] + [
        lax.ppermute(near, "group", [(g, (g + step) % 4) for g in range(4)])
        for step in range(1, 4)
    ]
    which = (group_index - source // 2) % 4 * 2 + (dec_index ^ (source % 2))
    span_rows = lax.dynamic_index_in_dim(jnp.concatenate(around, 0), which, 0, keepdims=False)
    span_part = attend_span(bundle, span_rows)

    own = merge(
        [low[0]],
        [from_up, from_down, span_part],
        [four] * 3 + [(4, LAST, NQ)],
        [
            ([[(0, t), (1, t), (2, t), (3, t)]], 0, NQ, *((True,) if t else ()))
            for t in range(4)
        ],
        rows,
    )
    x_received = [shift(own[2], 0, 1), shift(own[1], 0, -1), shift(own[3], 0, 2)]

    from_right = shift(right_sum, 0, -1)
    from_left = shift(left_sum, 0, 1)
    every = lambda t: [[(0, t), (1, t), (2, t)]]
    mine, rise1, fall1, rise2, fall2, rise3, fall3, far_up, far_down = merge(
        [wide[0]],
        [from_right, from_left],
        [eight] * 3,
        [(every(t), 0, NQ) for t in range(7)] + [(every(7), 0, SPLIT), (every(7), SPLIT, NQ)],
    )
    unit = (1, 0, NQ)
    pair = [([[(0, 0), (2, 0)]], 0, NQ), ([[(1, 0), (3, 0)]], 0, NQ)]
    rise_sum, fall_sum = merge(
        [],
        [rise3, fall3, shift(far_up, -1, 0), shift(far_down, 1, 0)],
        [unit, unit, (1, 0, SPLIT), (1, SPLIT, NQ)],
        pair,
    )
    for rise_own, fall_own in ((rise2, fall2), (rise1, fall1)):
        rise_sum, fall_sum = merge(
            [],
            [rise_own, fall_own, shift(rise_sum, -1, 0), shift(fall_sum, 1, 0)],
            [unit] * 4,
            pair,
        )
    s_messages = [mine, shift(rise_sum, -1, 0), shift(fall_sum, 1, 0), fresh_s]

    new_rows = unpack(
        x_index.reshape(1), rows, [x_received[1], x_received[2], x_received[0]]
    )
    attended = conclude(order, [own[0], *x_received, fresh_x], s_messages, value_absorb)
    return (new_rows, attended.reshape(REQS, 4, 4, 128))


def solution(mesh):
    return jax.shard_map(
        per_device,
        mesh=mesh,
        in_specs=(
            P(("group", "dec"), "tp"),
            P("tp"),
            P("tp", None),
            P(),
            P(),
            P(),
            P(("group", "dec"), "tp", None),
            P(("group", "dec"), None, "tp", None),
            P(("group", "dec"), None, "tp", None),
            P(("group", "dec"), None, None),
            P("tp", None, None),
            P("tp", None, None),
        ),
        out_specs=(P(("group", "dec"), None), P(("group", "dec"), None, "tp", None)),
        check_vma=False,
    )
```
